256 devices in a mesh: samp: 16 (over z_hi, x), row: 4 (over y), col: 4 (over z_lo, core).
Axes of the slice: x: 4, y: 4, z: 8 (z_hi: 4, z_lo: 2; z = z_hi * 2 + z_lo), core: 2. Of those that a mesh axis runs over, the one named last changes fastest.
Arguments:
- pair_in: bfloat16 [128, 512, 512], P(None, 'row', 'col'), may hold values from -6 to 6
- token_act: bfloat16 [48, 512, 768], P('samp', 'row', 'col'), may hold values from -6 to 6
- single: bfloat16 [512, 384], P('row'), may hold values from -6 to 6
- noise_sigma: float32 [48], P('samp'), may hold values from 0.05 to 80
- token_mask: int32 [512], P('row'), may hold values 0 or 1
- tri_weight: bfloat16 [5, 128, 128], replicated, may hold values from -0.5 to 0.5
- out_weight: bfloat16 [128, 128], replicated, may hold values from -0.5 to 0.5
- bias_weight: bfloat16 [2, 128, 16], replicated, may hold values from -2 to 2
- time_weight: bfloat16 [256, 384], replicated, may hold values from -0.375 to 0.375
- mod_weight: bfloat16 [2, 6, 384, 768], P(None, None, None, 'col'), may hold values from -0.3125 to 0.3125
- query_weight: bfloat16 [2, 768, 768], P(None, None, 'col'), may hold values from -2 to 2
- key_weight: bfloat16 [2, 768, 768], P(None, None, 'col'), may hold values from -2 to 2
- value_gate_weight: bfloat16 [2, 2, 768, 768], P(None, None, None, 'col'), may hold values from -0.21875 to 0.21875
- attn_out_weight: bfloat16 [2, 768, 768], P(None, 'col'), may hold values from -0.21875 to 0.21875
- up_weight: bfloat16 [2, 2, 768, 1536], P(None, None, None, 'col'), may hold values from -0.21875 to 0.21875
- down_weight: bfloat16 [2, 1536, 768], P(None, 'col'), may hold values from -0.15625 to 0.15625
Outputs:
- pair_out: bfloat16 [128, 512, 512], P('samp', 'row', 'col')
- denoised: bfloat16 [48, 512, 768], P('samp', 'row', 'col')
The draws below stay inside these ranges and needn't reach their ends.
Inputs may be any that keep to these rules, and one draw needn't show every extreme that they name: `token_mask`: 1 marks a token that queries attend to, 0 one that is left out.
All inputs are finite; a program needn't handle non-finite values. No bound on the sum of `token_mask` on one device may be relied on, other than what follows from the above.
Results may differ from the reference program's by a relative error of at most 0.019.
Values may be sent and summed in bfloat16 or wider, within the bound.
No kernel may reach another device: no remote copies, remote signals or barrier semaphores. Data moves between devices by JAX's collectives and lax.ppermute only.
A program may use at most 128 MiB of HBM per device.

```python
import math
import jax
import jax.numpy as jnp
from jax import lax

C = 128
DS = 384
DA = 768
HEADS = 16
HEAD_DIM = 48
TRANS_HIDDEN = 1536
TEMB = 256
BLOCKS = 2
TOKENS = 512
SAMPLES = 48


def draw_query_weight(key, part):
    key = jax.random.fold_in(key, 11)
    matrix = jax.random.normal(key, (BLOCKS, DA, DA), jnp.float32) * DA ** (-0.5)
    return jnp.clip(matrix, -2.0, 2.0).astype(jnp.bfloat16)


def draw_key_weight(key, part):
    key = jax.random.fold_in(key, 23)
    matrix = jax.random.normal(key, (BLOCKS, DA, DA), jnp.float32) * DA ** (-0.5)
    return jnp.clip(matrix, -2.0, 2.0).astype(jnp.bfloat16)


def touch_ends(drawn, key, low, largest):
    longest = drawn.shape.index(max(drawn.shape))
    spots = []
    for shift in (0, 1):
        where = [jax.random.randint(jax.random.fold_in(key, axis), (), 0, length) for axis, length in enumerate(drawn.shape)]
        where[longest] = (where[longest] + shift) % drawn.shape[longest]
        spots.append(tuple(where))
    return drawn.at[spots[0]].set(low).at[spots[1]].set(largest)


def block_scale(key, dims, pieces, smallest, largest):
    level, own = 1.0, jax.random.fold_in(key, 6)
    for axis_at, parts in pieces:
        draws = jnp.exp(jax.random.uniform(jax.random.fold_in(own, axis_at), (parts,), jnp.float32, smallest / len(pieces), largest / len(pieces)))
        level = level * jnp.repeat(draws, dims[axis_at] // parts).reshape([-1 if axis == axis_at else 1 for axis in range(len(dims))])
    return level


def scatter_about(key, shape, width, reach, cuts=(), held_as=jnp.bfloat16):
    result = jax.random.normal(key, shape, jnp.float32) * width
    if len(cuts) > 0:
        result = block_scale(key, shape, cuts, -0.22, 0.18) * result
    return jnp.clip(result, min=-reach, max=reach).astype(held_as)


def setup_inputs(seed: int = 0) -> dict:
    key_of = jax.random.split(jax.random.key(seed), 17)
    return {
        "pair_in": scatter_about(key_of[0], (C, TOKENS, TOKENS), 1.0, 6.0, ((1, 4), (2, 4))),
        "token_act": scatter_about(key_of[1], (SAMPLES, TOKENS, DA), 1.0, 6.0, ((0, 16), (1, 4), (2, 4))),
        "single": scatter_about(key_of[2], (TOKENS, DS), 1.0, 6.0, ((0, 4),)),
        "noise_sigma": jnp.clip(jnp.exp(math.log(80.0) - 7.377759 * jax.random.uniform(key_of[3], (SAMPLES,), jnp.float32) ** block_scale(key_of[3], (SAMPLES,), ((0, 16),), -0.2, 0.2)), 0.05, 80.0),
        "token_mask": touch_ends((jax.random.randint(key_of[4], (TOKENS,), 0, 8) < 7).astype(jnp.int32), jax.random.fold_in(key_of[4], 1), 0, 1),
        "tri_weight": scatter_about(key_of[5], (5, C, C), C ** -0.5, 0.5),
        "out_weight": scatter_about(key_of[6], (C, C), C ** -0.5, 0.5),
        "bias_weight": scatter_about(key_of[7], (BLOCKS, C, HEADS), (C // 16) ** -0.5, 2.0),
        "time_weight": scatter_about(key_of[8], (TEMB, DS), TEMB ** -0.5, 0.375),
        "mod_weight": scatter_about(key_of[9], (BLOCKS, 6, DS, DA), DS ** -0.5, 0.3125, ((3, 4),)),
        "query_weight": draw_query_weight(jax.random.fold_in(key_of[16], 71), 0),
        "key_weight": draw_key_weight(jax.random.fold_in(key_of[16], 71), 0),
        "value_gate_weight": scatter_about(key_of[12], (BLOCKS, 2, DA, DA), DA ** -0.5, 0.21875, ((3, 4),)),
        "attn_out_weight": scatter_about(key_of[13], (BLOCKS, DA, DA), DA ** -0.5, 0.21875, ((1, 4),)),
        "up_weight": scatter_about(key_of[14], (BLOCKS, 2, DA, TRANS_HIDDEN), DA ** -0.5, 0.21875, ((3, 4),)),
        "down_weight": scatter_about(key_of[15], (BLOCKS, TRANS_HIDDEN, DA), TRANS_HIDDEN ** -0.5, 0.15625, ((1, 4),)),
    }


EPS = 1e-05
MASK_FILL = 1000000000.0

def channel_norm(values, axis):
    mean_value = lax.optimization_barrier(jnp.mean(values, axis=axis, keepdims=True))
    centred = values - mean_value
    spread = lax.optimization_barrier(jnp.mean(centred * centred, axis=axis, keepdims=True))
    return centred * lax.rsqrt(spread + EPS)

def narrow(values):
    return values.astype(jnp.bfloat16)

def widened(values):
    return lax.optimization_barrier(values.astype(jnp.bfloat16)).astype(jnp.float32)

def reference(pair_in, token_act, single, noise_sigma, token_mask, tri_weight, out_weight, bias_weight, time_weight, mod_weight, query_weight, key_weight, value_gate_weight, attn_out_weight, up_weight, down_weight):
    pair_wide = pair_in.astype(jnp.float32)
    normed_pair = widened(channel_norm(pair_wide, 0))
    projected = []
    for proj_index in range(5):
        projected.append(jnp.einsum('cij,cd->dij', normed_pair, tri_weight[proj_index].astype(jnp.float32)))
    left_rows = widened(jax.nn.sigmoid(projected[0]) * projected[1])
    right_rows = widened(jax.nn.sigmoid(projected[2]) * projected[3])
    out_gate = jax.nn.sigmoid(projected[4])
    triangle_sum = jnp.einsum('cik,cjk->cij', left_rows, right_rows)
    triangle_normed = widened(channel_norm(triangle_sum, 0))
    pair_update = jnp.einsum('cij,co->oij', triangle_normed, out_weight.astype(jnp.float32))
    pair_out = narrow(pair_wide + out_gate * pair_update)
    pair_normed = widened(channel_norm(pair_out.astype(jnp.float32), 0))
    pair_bias = narrow(jnp.einsum('cij,bch->bhij', pair_normed, bias_weight.astype(jnp.float32)))
    half_count = TEMB // 2
    frequency = jnp.exp(jnp.arange(half_count, dtype=jnp.float32) * (math.log(100.0) / half_count))
    mask_add = (token_mask.astype(jnp.float32) - 1.0) * MASK_FILL
    score_scale = 1.0 / math.sqrt(HEAD_DIM)

    def denoise(inputs):
        sample_act, sample_sigma = inputs
        angles = jnp.log(sample_sigma) * 0.25 * frequency
        time_embed = narrow(jnp.concatenate([jnp.cos(angles), jnp.sin(angles)], 0))
        time_shift = jnp.dot(time_embed[None, :], time_weight, preferred_element_type=jnp.float32)
        condition = single.astype(jnp.float32) + time_shift
        cond_normed = widened(channel_norm(condition, 1))
        act_state = sample_act.astype(jnp.float32)
        for layer_index in range(BLOCKS):
            modulation = jnp.einsum('nd,mdf->mnf', cond_normed, mod_weight[layer_index].astype(jnp.float32))
            act_normed = channel_norm(act_state, 1)
            attn_in = narrow(jax.nn.sigmoid(modulation[0]) * act_normed + modulation[1])
            trans_in = narrow(jax.nn.sigmoid(modulation[2]) * act_normed + modulation[3])
            queries = widened(jnp.dot(attn_in, query_weight[layer_index], preferred_element_type=jnp.float32)).reshape(TOKENS, HEADS, HEAD_DIM)
            key_rows = widened(jnp.dot(attn_in, key_weight[layer_index], preferred_element_type=jnp.float32)).reshape(TOKENS, HEADS, HEAD_DIM)
            values = widened(jnp.dot(attn_in, value_gate_weight[layer_index, 0], preferred_element_type=jnp.float32)).reshape(TOKENS, HEADS, HEAD_DIM)
            gate_rows = widened(jnp.dot(attn_in, value_gate_weight[layer_index, 1], preferred_element_type=jnp.float32)).reshape(TOKENS, HEADS, HEAD_DIM)
            scores = jnp.einsum('qhe,khe->hqk', queries, key_rows) * score_scale
            scores = scores + pair_bias[layer_index].astype(jnp.float32) + mask_add[None, None, :]
            row_peak = lax.optimization_barrier(jnp.max(scores, axis=2, keepdims=True))
            exps = jnp.exp(scores - row_peak)
            denominator = lax.optimization_barrier(jnp.sum(exps, axis=2))
            weights = widened(exps)
            summed = jnp.einsum('hqk,khe->qhe', weights, values)
            attended = narrow(jax.nn.sigmoid(gate_rows) * summed / jnp.transpose(denominator)[:, :, None]).reshape(TOKENS, DA)
            attn_branch = jnp.dot(attended, attn_out_weight[layer_index], preferred_element_type=jnp.float32)
            swish_part = jnp.dot(trans_in, up_weight[layer_index, 0], preferred_element_type=jnp.float32)
            linear_part = jnp.dot(trans_in, up_weight[layer_index, 1], preferred_element_type=jnp.float32)
            hidden = narrow(jax.nn.silu(swish_part) * linear_part)
            trans_branch = jnp.dot(hidden, down_weight[layer_index], preferred_element_type=jnp.float32)
            act_state = jax.nn.sigmoid(modulation[4]) * attn_branch + jax.nn.sigmoid(modulation[5]) * trans_branch
        return narrow(act_state)
    denoised = lax.map(denoise, (token_act, noise_sigma))
    return (pair_out, denoised)
```

```python
import math

import jax
import jax.numpy as jnp
from jax import lax
from jax.sharding import PartitionSpec as P

DA = 768
HEAD_DIM = 48
TEMB = 256


EPS = 1e-05
MASK_FILL = 1000000000.0


def channel_norm(values, axis):
    mean_value = jnp.mean(values, axis=axis, keepdims=True)
    centred = values - mean_value
    spread = jnp.mean(centred * centred, axis=axis, keepdims=True)
    return centred * lax.rsqrt(spread + EPS)


def shared_norm(values, total_sum, total_square, entries):
    mean_value = total_sum / entries
    spread = total_square / entries - mean_value * mean_value
    return (values - mean_value) * lax.rsqrt(spread + EPS)

def sum_norm(values, axis, entries):
    mean_value = jnp.sum(values, axis=axis, keepdims=True) / entries
    centred = values - mean_value
    spread = jnp.sum(centred * centred, axis=axis, keepdims=True) / entries
    return centred * lax.rsqrt(spread + EPS)


def swap(value, axis, flip):
    size = lax.axis_size(axis)
    return lax.ppermute(value, axis, [(k, k ^ flip) for k in range(size)])


def swap_all(value, axis):
    return [value] + [swap(value, axis, flip) for flip in range(1, lax.axis_size(axis))]


def in_order(blocks, axis):
    me = lax.axis_index(axis)
    held = jnp.zeros((len(blocks),) + blocks[0].shape, blocks[0].dtype)
    for flip, block in enumerate(blocks):
        held = lax.dynamic_update_slice_in_dim(held, block[None], me ^ flip, 0)
    return held


def rows_by_flip(weight, axis):
    me, size = lax.axis_index(axis), lax.axis_size(axis)
    depth = weight.shape[0] // size
    return jnp.concatenate(
        [lax.dynamic_slice_in_dim(weight, (me ^ k) * depth, depth, 0) for k in range(size)], 0
    )


def swap_samp(value, step):
    return lax.ppermute(value, "samp", [(k, k ^ step) for k in range(lax.axis_size("samp"))])


def spread_bias(part):
    me = lax.axis_index("samp")
    blocks = [part] + [swap_samp(part, 4 * k) for k in range(1, 4)]
    near = jnp.zeros((4,) + part.shape, part.dtype)
    for k, block in enumerate(blocks):
        near = lax.dynamic_update_slice_in_dim(near, block[None], (me // 4) ^ k, 0)
    wide = [near] + [swap_samp(near, k) for k in range(1, 4)]
    held = jnp.zeros((4, 4) + part.shape, part.dtype)
    for k, block in enumerate(wide):
        held = lax.dynamic_update_slice_in_dim(held, block[:, None], (me % 4) ^ k, 1)
    return held.reshape((16,) + part.shape)


def body(
    pair_in,
    token_act,
    single,
    noise_sigma,
    token_mask,
    tri_weight,
    out_weight,
    bias_weight,
    time_weight,
    mod_weight,
    query_weight,
    key_weight,
    value_gate_weight,
    attn_out_weight,
    up_weight,
    down_weight,
):
    channels, pair_rows, pair_cols = pair_in.shape
    samp_size, row_size, col_size = (lax.axis_size(name) for name in ("samp", "row", "col"))
    group = row_size * col_size
    share = channels // samp_size
    halves = group // share
    half_rows = pair_rows // halves
    samp_at = lax.axis_index("samp")
    col_at = lax.axis_index("col")
    blocks, _, head_count = bias_weight.shape

    normed_pair = channel_norm(pair_in.astype(jnp.float32), 0).astype(jnp.bfloat16)
    local_weight = lax.dynamic_slice_in_dim(tri_weight[:4], samp_at * share, share, 2)
    projected = jnp.einsum(
        "cij,pcd->pdij", normed_pair, local_weight, preferred_element_type=jnp.float32
    )
    left_rows = (jax.nn.sigmoid(projected[0]) * projected[1]).astype(jnp.bfloat16)
    right_rows = (jax.nn.sigmoid(projected[2]) * projected[3]).astype(jnp.bfloat16)
    to_send = jnp.concatenate(
        [
            left_rows.reshape(group, half_rows, pair_cols),
            jnp.broadcast_to(
                right_rows[:, None], (share, halves, pair_rows, pair_cols)
            ).reshape(group, pair_rows, pair_cols),
        ],
        1,
    )
    came = lax.all_to_all(to_send, ("row", "col"), 0, 0, tiled=True)
    came = came.reshape(row_size, col_size, half_rows + pair_rows, pair_cols)
    triangle = jnp.einsum(
        "acik,bcjk->aibj",
        came[:, :, :half_rows],
        came[:, :, half_rows:],
        preferred_element_type=jnp.float32,
    ).astype(jnp.bfloat16)
    cell_rows = half_rows // samp_size
    triangle = triangle.reshape(row_size, cell_rows, samp_size, col_size, pair_cols)
    triangle = jnp.transpose(triangle, (2, 0, 3, 1, 4)).reshape(
        samp_size * group, cell_rows, pair_cols
    )
    triangle = lax.all_to_all(triangle, ("samp", "row", "col"), 0, 0, tiled=True)
    own_rows = halves * cell_rows
    triangle = triangle.reshape(channels, own_rows, pair_cols).astype(jnp.float32)

    own_pair = lax.dynamic_slice_in_dim(
        pair_in.reshape(channels, own_rows, samp_size, pair_cols), samp_at, 1, 2
    )[:, :, 0].astype(jnp.float32)
    own_normed = channel_norm(own_pair, 0).astype(jnp.bfloat16)
    out_gate = jax.nn.sigmoid(
        jnp.einsum("cuj,cd->duj", own_normed, tri_weight[4], preferred_element_type=jnp.float32)
    )
    triangle_normed = channel_norm(triangle, 0).astype(jnp.bfloat16)
    pair_update = jnp.einsum(
        "cuj,co->ouj", triangle_normed, out_weight, preferred_element_type=jnp.float32
    )
    pair_out = (own_pair + out_gate * pair_update).astype(jnp.bfloat16)
    pair_normed = channel_norm(pair_out.astype(jnp.float32), 0).astype(jnp.bfloat16)
    pair_bias = jnp.einsum(
        "cuj,bch->bhuj", pair_normed, bias_weight, preferred_element_type=jnp.float32
    ).astype(jnp.bfloat16)
    head_bias = lax.all_to_all(pair_bias, "col", split_axis=1, concat_axis=3, tiled=True)
    spread = [spread_bias(head_bias[layer]) for layer in range(blocks)]

    pair_back = lax.all_to_all(
        pair_out.reshape(samp_size, share, own_rows, pair_cols), "samp", 0, 0, tiled=True
    )
    pair_back = jnp.transpose(pair_back, (1, 2, 0, 3)).reshape(share, pair_rows, pair_cols)

    samples, row_count, width = token_act.shape
    heads_local = head_count // col_size
    half_count = TEMB // 2
    frequency = jnp.exp(jnp.arange(half_count, dtype=jnp.float32) * (math.log(100.0) / half_count))
    angles = (jnp.log(noise_sigma) * 0.25)[:, None] * frequency[None, :]
    time_embed = jnp.concatenate([jnp.cos(angles), jnp.sin(angles)], 1).astype(jnp.bfloat16)
    time_shift = jnp.dot(time_embed, time_weight, preferred_element_type=jnp.float32)
    condition = single.astype(jnp.float32)[None] + time_shift[:, None, :]
    cond_normed = channel_norm(condition, 2).astype(jnp.bfloat16)
    modulation = jnp.einsum(
        "snd,bmdf->bmsnf", cond_normed, mod_weight, preferred_element_type=jnp.float32
    )
    mask_add = (token_mask.astype(jnp.float32) - 1.0) * MASK_FILL
    mask_all = in_order(swap_all(mask_add[None], "row"), "row").reshape(-1)
    out_parts = [
        swap(
            lax.dynamic_slice_in_dim(attn_out_weight, (col_at ^ k) * width, width, 2), "col", k
        )
        for k in range(1, col_size)
    ]
    out_parts = [lax.dynamic_slice_in_dim(attn_out_weight, col_at * width, width, 2)] + out_parts
    out_columns = in_order(out_parts, "col")

    score_scale = 1.0 / math.sqrt(HEAD_DIM)
    act_state = token_act.astype(jnp.float32)
    for layer_index in range(blocks):
        layer_mod = modulation[layer_index]
        sums = jnp.stack([jnp.sum(act_state, 2), jnp.sum(act_state * act_state, 2)])
        sums = sum(swap_all(sums, "col"))
        act_normed = shared_norm(act_state, sums[0][:, :, None], sums[1][:, :, None], DA)
        attn_local = (jax.nn.sigmoid(layer_mod[0]) * act_normed + layer_mod[1]).astype(jnp.bfloat16)
        trans_local = (jax.nn.sigmoid(layer_mod[2]) * act_normed + layer_mod[3]).astype(
            jnp.bfloat16
        )
        joint_weight = jnp.concatenate(
            [
                query_weight[layer_index],
                key_weight[layer_index],
                value_gate_weight[layer_index, 0],
                value_gate_weight[layer_index, 1],
            ],
            1,
        )
        rise_weight = jnp.concatenate([up_weight[layer_index, 0], up_weight[layer_index, 1]], 1)
        if layer_index == 0:
            attn_full = jnp.concatenate(swap_all(attn_local, "col"), 2)
            trans_full = jnp.concatenate(swap_all(trans_local, "col"), 2)
            joint_weight = rows_by_flip(joint_weight, "col")
            rise_weight = rows_by_flip(rise_weight, "col")
        else:
            attn_full = lax.all_gather(attn_local, "col", axis=2, tiled=True)
            trans_full = lax.all_gather(trans_local, "col", axis=2, tiled=True)
        joint = jnp.einsum(
            "snd,df->snf", attn_full, joint_weight, preferred_element_type=jnp.float32
        ).astype(jnp.bfloat16)
        queries = joint[:, :, :width]
        gate_rows = joint[:, :, 3 * width :]
        both = in_order(swap_all(joint[:, :, width : 3 * width], "row"), "row")
        up_parts = jnp.einsum(
            "snd,df->snf", trans_full, rise_weight, preferred_element_type=jnp.float32
        )
        hidden_count = rise_weight.shape[1] // 2
        hidden = (jax.nn.silu(up_parts[:, :, :hidden_count]) * up_parts[:, :, hidden_count:]).astype(
            jnp.bfloat16
        )
        fall = down_weight[layer_index]
        trans_share = jnp.einsum(
            "snf,fd->snd",
            hidden,
            lax.dynamic_slice_in_dim(fall, col_at * width, width, 1),
            preferred_element_type=jnp.float32,
        )
        for k in range(1, col_size):
            part = jnp.einsum(
                "snf,fd->snd",
                hidden,
                lax.dynamic_slice_in_dim(fall, (col_at ^ k) * width, width, 1),
                preferred_element_type=jnp.float32,
            ).astype(jnp.bfloat16)
            trans_share = trans_share + swap(part, "col", k).astype(jnp.float32)
        layer_bias = jnp.transpose(spread[layer_index], (1, 2, 0, 3)).reshape(
            heads_local, row_count, -1
        )
        query_split = queries.reshape(samples, row_count, heads_local, HEAD_DIM)
        key_split = both[..., :width].reshape(row_size, samples, row_count, heads_local, HEAD_DIM)
        value_split = both[..., width:].reshape(row_size, samples, row_count, heads_local, HEAD_DIM)
        scores = jnp.einsum(
            "sqhe,rskhe->shqrk", query_split, key_split, preferred_element_type=jnp.float32
        ).reshape(samples, heads_local, row_count, -1)
        scores = scores * score_scale + layer_bias.astype(jnp.float32)[None] + mask_all
        exps = jnp.exp(scores - jnp.max(scores, axis=3, keepdims=True))
        total = jnp.sum(exps, axis=3)
        product = jnp.einsum(
            "shqrk,rskhe->shqe",
            exps.astype(jnp.bfloat16).reshape(samples, heads_local, row_count, row_size, row_count),
            value_split,
            preferred_element_type=jnp.float32,
        )
        product = jnp.transpose(product / total[..., None], (0, 2, 1, 3)).reshape(
            samples, row_count, width
        )
        attended = (jax.nn.sigmoid(gate_rows.astype(jnp.float32)) * product).astype(jnp.bfloat16)
        attended = lax.all_gather(attended, "col", axis=2, tiled=True)
        attn_share = jnp.einsum(
            "snf,fd->snd",
            attended,
            out_columns[:, layer_index].reshape(-1, width),
            preferred_element_type=jnp.float32,
        )
        act_state = (
            jax.nn.sigmoid(layer_mod[4]) * attn_share + jax.nn.sigmoid(layer_mod[5]) * trans_share
        )
    return (pair_back, act_state.astype(jnp.bfloat16))


def solution(mesh):
    placed = (
        P(None, "row", "col"),
        P("samp", "row", "col"),
        P("row", None),
        P("samp"),
        P("row"),
        P(),
        P(),
        P(),
        P(),
        P(None, None, None, "col"),
        P(None, None, "col"),
        P(None, None, "col"),
        P(None, None, None, "col"),
        P(None, "col", None),
        P(None, None, None, "col"),
        P(None, "col", None),
    )
    return jax.shard_map(
        body,
        mesh=mesh,
        in_specs=placed,
        out_specs=(P("samp", "row", "col"), P("samp", "row", "col")),
        check_vma=False,
    )
```

```python
import math

import jax
import jax.numpy as jnp
from jax import lax
from jax.experimental import pallas as pl
from jax.experimental.pallas import tpu as pltpu
from jax.sharding import PartitionSpec as P

DA = 768
HEAD_DIM = 48
TEMB = 256


EPS = 1e-05
MASK_FILL = 1000000000.0
VMEM_BYTES = 48 * 1024 * 1024
MASK_ROWS = 16


def channel_norm(values, axis):
    mean_value = jnp.mean(values, axis=axis, keepdims=True)
    centred = values - mean_value
    spread = jnp.mean(centred * centred, axis=axis, keepdims=True)
    return centred * lax.rsqrt(spread + EPS)


def swap(value, axis, flip):
    size = lax.axis_size(axis)
    return lax.ppermute(value, axis, [(k, k ^ flip) for k in range(size)])


def swap_all(value, axis):
    return [value] + [swap(value, axis, flip) for flip in range(1, lax.axis_size(axis))]


def local_call(kernel, out_shape, in_specs, args, scratch, flops, name):
    moved = sum(a.size * a.dtype.itemsize for a in args)
    return pl.pallas_call(
        kernel,
        grid=(1,),
        out_shape=out_shape,
        in_specs=in_specs,
        out_specs=jax.tree.map(lambda o: whole(o.shape), out_shape),
        scratch_shapes=scratch,
        compiler_params=pltpu.CompilerParams(vmem_limit_bytes=VMEM_BYTES),
        cost_estimate=pl.CostEstimate(flops=flops, bytes_accessed=moved, transcendentals=0),
        name=name,
    )(*args)


def whole(shape):
    return pl.BlockSpec(tuple(shape), lambda i: (0,) * len(shape))


def layer_block(shape, at, layer):
    block = tuple(1 if d == at else n for d, n in enumerate(shape))
    return pl.BlockSpec(block, lambda i: tuple(layer if d == at else 0 for d in range(len(shape))))


SCALAR = pl.BlockSpec(memory_space=pltpu.SMEM)


def stack_features(blocks, full, me):
    for k, block in enumerate(blocks):
        samples, width, tokens = block.shape
        start = pl.multiple_of((me ^ k) * width, width)
        for s in range(samples):
            full[pl.ds(start, width), s * tokens : (s + 1) * tokens] = block[s]


def stack_gathered(gathered, full):
    parts, samples, width, tokens = gathered.shape
    for k in range(parts):
        for s in range(samples):
            full[k * width : (k + 1) * width, s * tokens : (s + 1) * tokens] = gathered[k, s]


def fill(blocks, full, me):
    if len(blocks) == 1:
        stack_gathered(blocks[0], full)
    else:
        stack_features(blocks, full, me)


def project_kernel(count, me_ref, *refs):
    blocks = refs[:count]
    query_w, key_w, value_gate_w, mask, queries, gates, both, full = refs[count:]
    fill(blocks, full, me_ref[0])
    samples, width, tokens = queries.shape

    def times(weight):
        return jnp.dot(weight, full[...], preferred_element_type=jnp.float32).astype(jnp.bfloat16)

    query, gate = times(query_w[0]), times(value_gate_w[0, 1])
    key, value = times(key_w[0]), times(value_gate_w[0, 0])
    for s in range(samples):
        at = slice(s * tokens, (s + 1) * tokens)
        queries[s] = query[:, at]
        gates[s] = gate[:, at]
        both[2 * s * width : (2 * s + 1) * width] = key[:, at]
        both[(2 * s + 1) * width : (2 * s + 2) * width] = value[:, at]
    both[2 * samples * width :] = jnp.broadcast_to(mask[...], (MASK_ROWS, tokens))


def project(blocks, me, query_w, key_w, value_gate_w, mask, layer):
    samples, width, tokens = blocks[0].shape[-3:]
    small = jax.ShapeDtypeStruct((samples, width, tokens), jnp.bfloat16)
    joint = jax.ShapeDtypeStruct((2 * samples * width + MASK_ROWS, tokens), jnp.bfloat16)
    depth = query_w.shape[2]
    return local_call(
        lambda *refs: project_kernel(len(blocks), *refs),
        (small, small, joint),
        [SCALAR]
        + [whole(b.shape) for b in blocks]
        + [
            layer_block(query_w.shape, 0, layer),
            layer_block(key_w.shape, 0, layer),
            layer_block(value_gate_w.shape, 0, layer),
            whole(mask.shape),
        ],
        [me, *blocks, query_w, key_w, value_gate_w, mask],
        [pltpu.VMEM((depth, samples * tokens), jnp.bfloat16)],
        8 * depth * width * samples * tokens,
        "project",
    )


def transition_kernel(count, me_ref, *refs):
    blocks = refs[:count]
    up, down, own, parts, full, total = refs[count:]
    me = me_ref[0]
    fill(blocks, full, me)
    samples, width, tokens = own.shape
    over_rows = (((0,), (0,)), ((), ()))
    swish = lax.dot_general(up[0, 0], full[...], over_rows, preferred_element_type=jnp.float32)
    linear = lax.dot_general(up[0, 1], full[...], over_rows, preferred_element_type=jnp.float32)
    hidden = (swish / (1.0 + jnp.exp(-swish)) * linear).astype(jnp.bfloat16)
    total[...] = lax.dot_general(down[0], hidden, over_rows, preferred_element_type=jnp.float32)
    for k in range(parts.shape[0] + 1):
        start = pl.multiple_of((me ^ k) * width, width)
        for s in range(samples):
            piece = total[pl.ds(start, width), s * tokens : (s + 1) * tokens]
            if k == 0:
                own[s] = piece
            else:
                parts[k - 1, s] = piece.astype(jnp.bfloat16)


def transition(blocks, me, up, down, layer, col_size):
    samples, width, tokens = blocks[0].shape[-3:]
    depth, hidden = up.shape[2:]
    return local_call(
        lambda *refs: transition_kernel(len(blocks), *refs),
        (
            jax.ShapeDtypeStruct((samples, width, tokens), jnp.float32),
            jax.ShapeDtypeStruct((col_size - 1, samples, width, tokens), jnp.bfloat16),
        ),
        [SCALAR]
        + [whole(b.shape) for b in blocks]
        + [layer_block(up.shape, 0, layer), layer_block(down.shape, 0, layer)],
        [me, *blocks, up, down],
        [
            pltpu.VMEM((depth, samples * tokens), jnp.bfloat16),
            pltpu.VMEM((depth, samples * tokens), jnp.float32),
        ],
        6 * depth * hidden * samples * tokens,
        "transition",
    )


def attention_kernel(me_ref, queries, gates, kv0, kv1, kv2, kv3, bias, out):
    pieces = (kv0, kv1, kv2, kv3)
    me = me_ref[0]
    samples, width, tokens = queries.shape
    heads = bias.shape[2]
    scale = 1.0 / math.sqrt(HEAD_DIM)
    lane = lax.broadcasted_iota(jnp.int32, (tokens, width), 1) // HEAD_DIM
    masks = jnp.concatenate(
        [kv[2 * samples * width : 2 * samples * width + 1].astype(jnp.float32) for kv in pieces], 1
    )
    mask_add = (masks - 1.0) * MASK_FILL
    for s in range(samples):
        query = jnp.transpose(queries[s].astype(jnp.float32))
        key = jnp.concatenate([kv[2 * s * width : (2 * s + 1) * width] for kv in pieces], 1)
        value = jnp.concatenate([kv[(2 * s + 1) * width : (2 * s + 2) * width] for kv in pieces], 1)
        kept = jnp.zeros((tokens, width), jnp.float32)
        for h in range(heads):
            mine = lane == h
            scores = jnp.dot(
                jnp.where(mine, query, 0.0).astype(jnp.bfloat16),
                key,
                preferred_element_type=jnp.float32,
            )
            added = jnp.concatenate(
                [
                    bias[:, me ^ k, h].astype(jnp.float32).reshape(tokens, tokens)
                    for k in range(len(pieces))
                ],
                1,
            )
            scores = scores * scale + added + mask_add
            exps = jnp.exp(scores - jnp.max(scores, axis=1, keepdims=True))
            total = jnp.sum(exps, axis=1, keepdims=True)
            product = lax.dot_general(
                exps.astype(jnp.bfloat16),
                value,
                (((1,), (1,)), ((), ())),
                preferred_element_type=jnp.float32,
            )
            kept = jnp.where(mine, product / total, kept)
        gate = jax.nn.sigmoid(gates[s].astype(jnp.float32))
        out[s] = (gate * jnp.transpose(kept)).astype(jnp.bfloat16)


def attention(me, queries, gates, pieces, bias):
    samples, width, tokens = queries.shape
    args = [me, queries, gates, *pieces, bias]
    return local_call(
        attention_kernel,
        jax.ShapeDtypeStruct(queries.shape, jnp.bfloat16),
        [SCALAR] + [whole(a.shape) for a in args[1:]],
        args,
        [],
        4 * samples * bias.shape[2] * tokens * tokens * len(pieces) * width,
        "attention",
    )


def finish_kernel(attended, out_w, own, came0, came1, came2, gate_a, gate_t, state, full):
    stack_gathered(attended, full)
    samples, width, tokens = own.shape
    total = jnp.zeros((width, samples * tokens), jnp.float32)
    for k in range(attended.shape[0]):
        total = total + lax.dot_general(
            out_w[k, 0],
            full[k * width : (k + 1) * width],
            (((0,), (0,)), ((), ())),
            preferred_element_type=jnp.float32,
        )
    for s in range(samples):
        trans = own[s]
        for came in (came0, came1, came2):
            trans = trans + came[s].astype(jnp.float32)
        branch = total[:, s * tokens : (s + 1) * tokens]
        value = gate_a[0, 0, s] * branch + gate_t[0, 0, s] * trans
        state[s] = value.astype(state.dtype)


def finish(attended, out_w, own, came, mods, layer, out_type):
    samples, width, tokens = own.shape
    parts = attended.shape[0]

    def mod_block(m):
        return pl.BlockSpec((1, 1) + own.shape, lambda i: (layer, m, 0, 0, 0))

    return local_call(
        finish_kernel,
        jax.ShapeDtypeStruct(own.shape, out_type),
        [whole(attended.shape), layer_block(out_w.shape, 1, layer), whole(own.shape)]
        + [whole(c.shape) for c in came]
        + [mod_block(4), mod_block(5)],
        [attended, out_w, own, *came, mods, mods],
        [pltpu.VMEM((parts * width, samples * tokens), jnp.bfloat16)],
        2 * parts * width * width * samples * tokens,
        "finish",
    )


def modulate_kernel(single, shift, mod_w, out, normed):
    samples, width, tokens = out.shape[2:]

    @pl.when(pl.program_id(0) == 0)
    def _():
        for s in range(samples):
            condition = single[...].astype(jnp.float32) + shift[s : s + 1, :]
            normed[s * tokens : (s + 1) * tokens] = channel_norm(condition, 1).astype(jnp.bfloat16)

    for m in range(mod_w.shape[1]):
        made = lax.dot_general(
            mod_w[0, m], normed[...], (((1,), (1,)), ((), ())), preferred_element_type=jnp.float32
        )
        if m not in (1, 3):
            made = jax.nn.sigmoid(made)
        for s in range(samples):
            out[0, m, s] = made[:, s * tokens : (s + 1) * tokens]


def modulate(single, shift, mod_w):
    layers, count, width, depth = mod_w.shape
    tokens, samples = single.shape[0], shift.shape[0]
    return pl.pallas_call(
        modulate_kernel,
        grid=(layers,),
        out_shape=jax.ShapeDtypeStruct((layers, count, samples, width, tokens), jnp.float32),
        in_specs=[
            whole(single.shape),
            whole(shift.shape),
            pl.BlockSpec((1, count, width, depth), lambda i: (i, 0, 0, 0)),
        ],
        out_specs=pl.BlockSpec((1, count, samples, width, tokens), lambda i: (i, 0, 0, 0, 0)),
        scratch_shapes=[pltpu.VMEM((samples * tokens, depth), jnp.bfloat16)],
        compiler_params=pltpu.CompilerParams(vmem_limit_bytes=VMEM_BYTES),
        cost_estimate=pl.CostEstimate(
            flops=2 * layers * count * width * depth * samples * tokens,
            bytes_accessed=6 * mod_w.size,
            transcendentals=0,
        ),
        name="modulate",
    )(single, shift, mod_w)


def body(
    pair_in,
    token_act,
    single,
    noise_sigma,
    token_mask,
    tri_weight,
    out_weight,
    bias_weight,
    time_weight,
    mod_weight,
    query_weight,
    key_weight,
    value_gate_weight,
    attn_out_weight,
    up_weight,
    down_weight,
):
    channels, pair_rows, pair_cols = pair_in.shape
    samp_size, row_size, col_size = (lax.axis_size(name) for name in ("samp", "row", "col"))
    group = row_size * col_size
    share = channels // samp_size
    halves = group // share
    half_rows = pair_rows // halves
    cell_rows = half_rows // samp_size
    own_rows = halves * cell_rows
    samp_at = lax.axis_index("samp")
    row_at = jnp.reshape(lax.axis_index("row"), (1,))
    col_at = jnp.reshape(lax.axis_index("col"), (1,))
    blocks, _, head_count = bias_weight.shape
    heads_local = head_count // col_size

    normed_pair = channel_norm(pair_in.astype(jnp.float32), 0).astype(jnp.bfloat16)
    local_weight = lax.dynamic_slice_in_dim(tri_weight[:4], samp_at * share, share, 2)
    projected = jnp.einsum(
        "cij,pcd->pdij", normed_pair, local_weight, preferred_element_type=jnp.float32
    )
    left_rows = (jax.nn.sigmoid(projected[0]) * projected[1]).astype(jnp.bfloat16)
    right_rows = (jax.nn.sigmoid(projected[2]) * projected[3]).astype(jnp.bfloat16)
    left_rows = left_rows.reshape(share, samp_size, halves, cell_rows, pair_cols)
    to_send = jnp.concatenate(
        [
            jnp.transpose(left_rows, (0, 2, 1, 3, 4)).reshape(group, half_rows, pair_cols),
            jnp.broadcast_to(
                right_rows[:, None], (share, halves, pair_rows, pair_cols)
            ).reshape(group, pair_rows, pair_cols),
        ],
        1,
    )
    came = lax.all_to_all(to_send, ("row", "col"), 0, 0, tiled=True)
    came = came.reshape(row_size, col_size, half_rows + pair_rows, pair_cols)
    triangle = jnp.einsum(
        "acik,bcjk->aibj",
        came[:, :, :half_rows],
        came[:, :, half_rows:],
        preferred_element_type=jnp.float32,
    ).astype(jnp.bfloat16)
    triangle = triangle.reshape(row_size, samp_size, cell_rows, col_size, pair_cols)
    triangle = jnp.transpose(triangle, (1, 0, 3, 2, 4)).reshape(
        samp_size * group, cell_rows, pair_cols
    )
    triangle = lax.all_to_all(triangle, ("samp", "row", "col"), 0, 0, tiled=True)
    triangle = triangle.reshape(channels, own_rows, pair_cols).astype(jnp.float32)

    own_pair = lax.dynamic_slice_in_dim(pair_in, samp_at * own_rows, own_rows, 1).astype(
        jnp.float32
    )
    own_normed = channel_norm(own_pair, 0).astype(jnp.bfloat16)
    out_gate = jax.nn.sigmoid(
        jnp.einsum("cuj,cd->duj", own_normed, tri_weight[4], preferred_element_type=jnp.float32)
    )
    triangle_normed = channel_norm(triangle, 0).astype(jnp.bfloat16)
    pair_update = jnp.einsum(
        "cuj,co->ouj", triangle_normed, out_weight, preferred_element_type=jnp.float32
    )
    pair_out = (own_pair + out_gate * pair_update).astype(jnp.bfloat16)
    pair_normed = channel_norm(pair_out.astype(jnp.float32), 0).astype(jnp.bfloat16)
    pair_bias = jnp.einsum(
        "cuj,bch->bhuj", pair_normed, bias_weight, preferred_element_type=jnp.float32
    ).astype(jnp.bfloat16)
    spread = []
    for layer in range(blocks):
        parts = pair_bias[layer].reshape(col_size, heads_local, own_rows, pair_cols)
        parts = jnp.broadcast_to(parts[None], (samp_size,) + parts.shape)
        parts = lax.all_to_all(
            parts.reshape(samp_size * col_size, heads_local, own_rows, pair_cols),
            ("samp", "col"),
            0,
            0,
            tiled=True,
        )
        spread.append(
            parts.reshape(samp_size, col_size, heads_local, own_rows, pair_cols)
        )
    pair_back = lax.all_to_all(
        pair_out.reshape(samp_size, share, own_rows, pair_cols), "samp", 0, 0, tiled=True
    )
    pair_back = jnp.transpose(pair_back, (1, 0, 2, 3)).reshape(share, pair_rows, pair_cols)

    state = jnp.swapaxes(token_act, 1, 2).astype(jnp.float32)
    samples, width, row_count = state.shape
    query_w = jnp.swapaxes(query_weight, 1, 2)
    key_w = jnp.swapaxes(key_weight, 1, 2)
    value_gate_w = jnp.swapaxes(value_gate_weight, 2, 3)
    mod_w = jnp.swapaxes(mod_weight, 2, 3)
    out_w = attn_out_weight.reshape(blocks, width, col_size, width)
    out_w = lax.all_to_all(jnp.transpose(out_w, (2, 0, 1, 3)), "col", 0, 0, tiled=True)
    half_count = TEMB // 2
    frequency = jnp.exp(jnp.arange(half_count, dtype=jnp.float32) * (math.log(100.0) / half_count))
    angles = (jnp.log(noise_sigma) * 0.25)[:, None] * frequency[None, :]
    time_embed = jnp.concatenate([jnp.cos(angles), jnp.sin(angles)], 1).astype(jnp.bfloat16)
    time_shift = jnp.dot(time_embed, time_weight, preferred_element_type=jnp.float32)
    mods = modulate(single, time_shift, mod_w)
    mask_row = token_mask.astype(jnp.bfloat16)[None]

    for layer in range(blocks):
        sums = jnp.stack([jnp.sum(state, 1), jnp.sum(state * state, 1)])
        if layer == 0:
            sums = sum(swap_all(sums, "col"))
        else:
            sums = jnp.sum(lax.all_gather(sums, "col", axis=0), 0)
        mean_value = sums[0] / DA
        scale = lax.rsqrt(sums[1] / DA - mean_value * mean_value + EPS)
        normed = (state - mean_value[:, None, :]) * scale[:, None, :]
        attn_local = (mods[layer, 0] * normed + mods[layer, 1]).astype(jnp.bfloat16)
        trans_local = (mods[layer, 2] * normed + mods[layer, 3]).astype(jnp.bfloat16)
        if layer == 0:
            attn_full = swap_all(attn_local, "col")
            trans_full = swap_all(trans_local, "col")
        else:
            attn_full = [lax.all_gather(attn_local, "col", axis=0)]
            trans_full = [lax.all_gather(trans_local, "col", axis=0)]
        queries, gates, both = project(
            attn_full, col_at, query_w, key_w, value_gate_w, mask_row, layer
        )
        pieces = swap_all(both, "row")
        own, parts = transition(trans_full, col_at, up_weight, down_weight, layer, col_size)
        trans_came = [swap(parts[k - 1], "col", k) for k in range(1, col_size)]
        attended = attention(row_at, queries, gates, pieces, spread[layer])
        attended = lax.all_gather(attended, "col", axis=0)
        last = layer == blocks - 1
        state = finish(
            attended, out_w, own, trans_came, mods, layer, jnp.bfloat16 if last else jnp.float32
        )
    return (pair_back, jnp.swapaxes(state, 1, 2))


def solution(mesh):
    placed = (
        P(None, "row", "col"),
        P("samp", "row", "col"),
        P("row", None),
        P("samp"),
        P("row"),
        P(),
        P(),
        P(),
        P(),
        P(None, None, None, "col"),
        P(None, None, "col"),
        P(None, None, "col"),
        P(None, None, None, "col"),
        P(None, "col", None),
        P(None, None, None, "col"),
        P(None, "col", None),
    )
    return jax.shard_map(
        body,
        mesh=mesh,
        in_specs=placed,
        out_specs=(P("samp", "row", "col"), P("samp", "row", "col")),
        check_vma=False,
    )
```

```python
import math

import jax
import jax.numpy as jnp
from jax import lax
from jax.experimental import pallas as pl
from jax.experimental.pallas import tpu as pltpu
from jax.sharding import PartitionSpec as P

DA = 768
HEAD_DIM = 48
TEMB = 256


EPS = 1e-05
MASK_FILL = 1000000000.0
MIB = 1024 * 1024
CLAIM = 56
MASK_ROWS = 16


def channel_norm(values, axis):
    mean_value = jnp.mean(values, axis=axis, keepdims=True)
    centred = values - mean_value
    spread = jnp.mean(centred * centred, axis=axis, keepdims=True)
    return centred * lax.rsqrt(spread + EPS)


def swap(value, axis, flip):
    size = lax.axis_size(axis)
    return lax.ppermute(value, axis, [(k, k ^ flip) for k in range(size)])


def swap_all(value, axis):
    return [value] + [swap(value, axis, flip) for flip in range(1, lax.axis_size(axis))]


def local_call(kernel, out_shape, in_specs, args, scratch, flops, name, mib=CLAIM):
    moved = sum(a.size * a.dtype.itemsize for a in args)
    return pl.pallas_call(
        kernel,
        grid=(1,),
        out_shape=out_shape,
        in_specs=in_specs,
        out_specs=jax.tree.map(lambda o: whole(o.shape), out_shape),
        scratch_shapes=scratch,
        compiler_params=pltpu.CompilerParams(vmem_limit_bytes=mib * MIB),
        cost_estimate=pl.CostEstimate(flops=flops, bytes_accessed=moved, transcendentals=0),
        name=name,
    )(*args)


def whole(shape):
    return pl.BlockSpec(tuple(shape), lambda i: (0,) * len(shape))


def layer_block(shape, at, layer):
    block = tuple(1 if d == at else n for d, n in enumerate(shape))
    return pl.BlockSpec(block, lambda i: tuple(layer if d == at else 0 for d in range(len(shape))))


SCALAR = pl.BlockSpec(memory_space=pltpu.SMEM)
UNREAD = pl.BlockSpec(memory_space=pl.ANY)


def after(value, others):
    def kernel(*refs):
        refs[-1][...] = refs[0][...]

    return local_call(
        kernel,
        jax.ShapeDtypeStruct(value.shape, value.dtype),
        [whole(value.shape)] + [UNREAD] * len(others),
        [value, *others],
        [],
        0,
        "after",
    )


def stack_gathered(gathered, full):
    parts, samples, width, tokens = gathered.shape
    for k in range(parts):
        for s in range(samples):
            full[k * width : (k + 1) * width, s * tokens : (s + 1) * tokens] = gathered[k, s]


def stack_normed(gathered, shared, full, gain_at):
    parts, samples, width, tokens = gathered.shape
    for s in range(samples):
        value = jnp.concatenate([gathered[k, s] for k in range(parts)], 0).astype(jnp.float32)
        normed = channel_norm(value, 0)
        for k in range(parts):
            gain, shift = shared[k, gain_at, s], shared[k, gain_at + 1, s]
            piece = normed[k * width : (k + 1) * width]
            full[k * width : (k + 1) * width, s * tokens : (s + 1) * tokens] = (
                gain.astype(jnp.float32) * piece + shift.astype(jnp.float32)
            ).astype(jnp.bfloat16)


def fill(blocks, full, gain_at):
    if len(blocks) == 2:
        stack_normed(blocks[0], blocks[1], full, gain_at)
    else:
        stack_gathered(blocks[0], full)


def project_kernel(count, *refs):
    blocks = refs[:count]
    query_w, key_w, value_gate_w, mask, queries, gates, both, full = refs[count:]
    fill(blocks, full, 0)
    samples, width, tokens = queries.shape

    def times(weight):
        return jnp.dot(weight, full[...], preferred_element_type=jnp.float32).astype(jnp.bfloat16)

    query, gate = times(query_w[0]), times(value_gate_w[0, 1])
    key, value = times(key_w[0]), times(value_gate_w[0, 0])
    for s in range(samples):
        at = slice(s * tokens, (s + 1) * tokens)
        queries[s] = query[:, at]
        gates[s] = gate[:, at]
        both[2 * s * width : (2 * s + 1) * width] = key[:, at]
        both[(2 * s + 1) * width : (2 * s + 2) * width] = value[:, at]
    both[2 * samples * width :] = jnp.broadcast_to(mask[...], (MASK_ROWS, tokens))


def project(blocks, query_w, key_w, value_gate_w, mask, layer):
    samples, width, tokens = blocks[0].shape[-3:]
    small = jax.ShapeDtypeStruct((samples, width, tokens), jnp.bfloat16)
    joint = jax.ShapeDtypeStruct((2 * samples * width + MASK_ROWS, tokens), jnp.bfloat16)
    depth = query_w.shape[2]
    return local_call(
        lambda *refs: project_kernel(len(blocks), *refs),
        (small, small, joint),
        [whole(b.shape) for b in blocks]
        + [
            layer_block(query_w.shape, 0, layer),
            layer_block(key_w.shape, 0, layer),
            layer_block(value_gate_w.shape, 0, layer),
            whole(mask.shape),
        ],
        [*blocks, query_w, key_w, value_gate_w, mask],
        [pltpu.VMEM((depth, samples * tokens), jnp.bfloat16)],
        8 * depth * width * samples * tokens,
        "project",
    )


def transition_kernel(count, me_ref, *refs):
    blocks = refs[:count]
    up, down, own, parts, full, total = refs[count:]
    me = me_ref[0]
    fill(blocks, full, 2)
    samples, width, tokens = own.shape
    over_rows = (((0,), (0,)), ((), ()))
    swish = lax.dot_general(up[0, 0], full[...], over_rows, preferred_element_type=jnp.float32)
    linear = lax.dot_general(up[0, 1], full[...], over_rows, preferred_element_type=jnp.float32)
    hidden = (swish / (1.0 + jnp.exp(-swish)) * linear).astype(jnp.bfloat16)
    total[...] = lax.dot_general(down[0], hidden, over_rows, preferred_element_type=jnp.float32)
    for k in range(parts.shape[0] + 1):
        start = pl.multiple_of((me ^ k) * width, width)
        for s in range(samples):
            piece = total[pl.ds(start, width), s * tokens : (s + 1) * tokens]
            if k == 0:
                own[s] = piece
            else:
                parts[k - 1, s] = piece.astype(jnp.bfloat16)


def transition(blocks, me, up, down, layer, col_size):
    samples, width, tokens = blocks[0].shape[-3:]
    depth, hidden = up.shape[2:]
    return local_call(
        lambda *refs: transition_kernel(len(blocks), *refs),
        (
            jax.ShapeDtypeStruct((samples, width, tokens), jnp.float32),
            jax.ShapeDtypeStruct((col_size - 1, samples, width, tokens), jnp.bfloat16),
        ),
        [SCALAR]
        + [whole(b.shape) for b in blocks]
        + [layer_block(up.shape, 0, layer), layer_block(down.shape, 0, layer)],
        [me, *blocks, up, down],
        [
            pltpu.VMEM((depth, samples * tokens), jnp.bfloat16),
            pltpu.VMEM((depth, samples * tokens), jnp.float32),
        ],
        6 * depth * hidden * samples * tokens,
        "transition",
    )


def attention_kernel(me_ref, queries, gates, kv0, kv1, kv2, kv3, bias, *refs):
    out = refs[-1]
    pieces = (kv0, kv1, kv2, kv3)
    me = me_ref[0]
    samples, width, tokens = queries.shape
    heads = bias.shape[2]
    scale = 1.0 / math.sqrt(HEAD_DIM)
    lane = lax.broadcasted_iota(jnp.int32, (tokens, width), 1) // HEAD_DIM
    masks = jnp.concatenate(
        [kv[2 * samples * width : 2 * samples * width + 1].astype(jnp.float32) for kv in pieces], 1
    )
    mask_add = (masks - 1.0) * MASK_FILL
    for s in range(samples):
        query = jnp.transpose(queries[s].astype(jnp.float32))
        key = jnp.concatenate([kv[2 * s * width : (2 * s + 1) * width] for kv in pieces], 1)
        value = jnp.concatenate([kv[(2 * s + 1) * width : (2 * s + 2) * width] for kv in pieces], 1)
        kept = jnp.zeros((tokens, width), jnp.float32)
        for h in range(heads):
            mine = lane == h
            scores = jnp.dot(
                jnp.where(mine, query, 0.0).astype(jnp.bfloat16),
                key,
                preferred_element_type=jnp.float32,
            )
            added = jnp.concatenate(
                [
                    bias[:, me ^ k, h].astype(jnp.float32).reshape(tokens, tokens)
                    for k in range(len(pieces))
                ],
                1,
            )
            scores = scores * scale + added + mask_add
            exps = jnp.exp(scores - jnp.max(scores, axis=1, keepdims=True))
            total = jnp.sum(exps, axis=1, keepdims=True)
            product = lax.dot_general(
                exps.astype(jnp.bfloat16),
                value,
                (((1,), (1,)), ((), ())),
                preferred_element_type=jnp.float32,
            )
            kept = jnp.where(mine, product / total, kept)
        gate = jax.nn.sigmoid(gates[s].astype(jnp.float32))
        out[s] = (gate * jnp.transpose(kept)).astype(jnp.bfloat16)


def attention(me, queries, gates, pieces, bias, others):
    samples, width, tokens = queries.shape
    args = [me, queries, gates, *pieces, bias]
    return local_call(
        attention_kernel,
        jax.ShapeDtypeStruct(queries.shape, jnp.bfloat16),
        [SCALAR] + [whole(a.shape) for a in args[1:]] + [UNREAD] * len(others),
        args + others,
        [],
        4 * samples * bias.shape[2] * tokens * tokens * len(pieces) * width,
        "attention",
    )


def finish_kernel(attended, out_w, own, came0, came1, came2, gate_a, gate_t, state, full):
    stack_gathered(attended, full)
    samples, width, tokens = own.shape
    total = jnp.zeros((width, samples * tokens), jnp.float32)
    for k in range(attended.shape[0]):
        total = total + lax.dot_general(
            out_w[k, 0],
            full[k * width : (k + 1) * width],
            (((0,), (0,)), ((), ())),
            preferred_element_type=jnp.float32,
        )
    for s in range(samples):
        trans = own[s]
        for came in (came0, came1, came2):
            trans = trans + came[s].astype(jnp.float32)
        branch = total[:, s * tokens : (s + 1) * tokens]
        value = gate_a[0, s] * branch + gate_t[0, s] * trans
        state[s] = value.astype(state.dtype)


def finish(attended, out_w, own, came, mods, layer, gate_at, out_type):
    samples, width, tokens = own.shape
    parts = attended.shape[0]

    def mod_block(m):
        return pl.BlockSpec((1,) + own.shape, lambda i: (m, 0, 0, 0))

    return local_call(
        finish_kernel,
        jax.ShapeDtypeStruct(own.shape, out_type),
        [whole(attended.shape), layer_block(out_w.shape, 1, layer), whole(own.shape)]
        + [whole(c.shape) for c in came]
        + [mod_block(gate_at), mod_block(gate_at + 1)],
        [attended, out_w, own, *came, mods, mods],
        [pltpu.VMEM((parts * width, samples * tokens), jnp.bfloat16)],
        2 * parts * width * width * samples * tokens,
        "finish",
    )


def modulate_kernel(single, shift, mod_w, own, shared, normed):
    samples, width, tokens = own.shape[1:]
    layers, count = mod_w.shape[:2]
    for s in range(samples):
        condition = single[...].astype(jnp.float32) + shift[s : s + 1, :]
        normed[s * tokens : (s + 1) * tokens] = channel_norm(condition, 1).astype(jnp.bfloat16)
    kept = 0
    for layer in range(layers):
        for m in range(count):
            made = lax.dot_general(
                mod_w[layer, m],
                normed[...],
                (((1,), (1,)), ((), ())),
                preferred_element_type=jnp.float32,
            )
            if m not in (1, 3):
                made = jax.nn.sigmoid(made)
            for s in range(samples):
                piece = made[:, s * tokens : (s + 1) * tokens]
                if layer > 0 and m < 4:
                    shared[m, s] = piece.astype(jnp.bfloat16)
                else:
                    own[kept, s] = piece
            kept += layer == 0 or m >= 4


def modulate(single, shift, mod_w):
    layers, count, width, depth = mod_w.shape
    tokens, samples = single.shape[0], shift.shape[0]
    return local_call(
        modulate_kernel,
        (
            jax.ShapeDtypeStruct((count + 2, samples, width, tokens), jnp.float32),
            jax.ShapeDtypeStruct((4, samples, width, tokens), jnp.bfloat16),
        ),
        [whole(single.shape), whole(shift.shape), whole(mod_w.shape)],
        [single, shift, mod_w],
        [pltpu.VMEM((samples * tokens, depth), jnp.bfloat16)],
        2 * layers * count * width * depth * samples * tokens,
        "modulate",
    )


def triangle_kernel(came, *refs):
    out = refs[-1]
    rows, cols, _, keys = came.shape
    half = 8 * out.shape[0]

    def joined(at):
        return jnp.concatenate(
            [jnp.concatenate([came[r, c, at] for c in range(cols)], 1) for r in range(rows)], 0
        )

    sums = lax.dot_general(
        joined(slice(0, half)),
        joined(slice(half, half + keys)),
        (((1,), (1,)), ((), ())),
        preferred_element_type=jnp.float32,
    )
    groups = half // 8
    upper = lax.broadcasted_iota(jnp.int32, (groups, 8, keys), 1) < 4
    for r in range(rows):
        for c in range(0, cols, 2):
            one, two = (
                sums[r * half : (r + 1) * half, k * keys : (k + 1) * keys].reshape(groups, 8, keys)
                for k in (c, c + 1)
            )
            even = jnp.where(upper, one, pltpu.roll(two, 4, 1))
            odd = jnp.where(upper, pltpu.roll(one, 4, 1), two)
            out[:, 0, r, c // 2] = even.astype(jnp.bfloat16)
            out[:, 1, r, c // 2] = odd.astype(jnp.bfloat16)


def triangle_sums(came, others):
    rows, cols, height, keys = came.shape
    half = height - keys
    left = rows * half
    return local_call(
        triangle_kernel,
        jax.ShapeDtypeStruct((half // 8, 2, rows, cols // 2, 8, keys), jnp.bfloat16),
        [whole(came.shape)] + [UNREAD] * len(others),
        [came, *others],
        [],
        2 * left * rows * keys * cols * keys,
        "triangle_sums",
    )


def pair_project_kernel(me_ref, pair, tri, out, weight, normed, left, right):
    step = pl.program_id(0)
    channels, rows, keys = pair.shape
    height = rows * pl.num_programs(0)
    share = weight.shape[0] // 4
    halves = out.shape[0] // share
    part = out.shape[1] - keys
    group = 8 // halves

    @pl.when(step == 0)
    def _():
        mine = lax.broadcasted_iota(jnp.int32, (share, channels), 0) + me_ref[0] * share
        pick = mine == lax.broadcasted_iota(jnp.int32, (share, channels), 1)
        for p in range(4):
            weight[p * share : (p + 1) * share] = lax.dot_general(
                pick.astype(jnp.bfloat16),
                tri[p],
                (((1,), (1,)), ((), ())),
                preferred_element_type=jnp.float32,
            )

    value = pair[...].astype(jnp.float32)
    normed[...] = channel_norm(value, 0).reshape(channels * rows, keys)
    weights = weight[...].astype(jnp.bfloat16)
    for i in range(0, rows, 2):
        two = [normed[pl.ds(i + e, channels, stride=rows), :] for e in (0, 1)]
        made = jnp.dot(
            weights, jnp.concatenate(two, 1).astype(jnp.bfloat16), preferred_element_type=jnp.float32
        )
        made_left = jax.nn.sigmoid(made[:share]) * made[share : 2 * share]
        made_right = jax.nn.sigmoid(made[2 * share : 3 * share]) * made[3 * share :]
        for e in (0, 1):
            row, at = i + e, slice(e * keys, (e + 1) * keys)
            right[pl.ds(step * rows + row, share, stride=keys), :] = made_right[:, at]
            place = (row % 8) // group * part + row // 8 * group + row % group
            place = step * (rows // 8 * group) + place
            left[pl.ds(place, share, stride=keys), :] = made_left[:, at]

    @pl.when(step == pl.num_programs(0) - 1)
    def _():
        for c in range(share):
            whole_right = right[c * keys : (c + 1) * keys].astype(jnp.bfloat16)
            for h in range(halves):
                start = c * keys + h * part
                out[c * halves + h, :part] = left[start : start + part].astype(jnp.bfloat16)
                out[c * halves + h, part:] = whole_right


def pair_project(pair_in, tri_weight, me, group, samp_size):
    channels, height, keys = pair_in.shape
    share = channels // samp_size
    part = height // (group // share)
    rows = 16
    out = jax.ShapeDtypeStruct((group, part + height, keys), jnp.bfloat16)
    return pl.pallas_call(
        pair_project_kernel,
        grid=(height // rows,),
        out_shape=out,
        in_specs=[
            SCALAR,
            pl.BlockSpec((channels, rows, keys), lambda i: (0, i, 0)),
            whole(tri_weight.shape),
        ],
        out_specs=whole(out.shape),
        scratch_shapes=[
            pltpu.VMEM((4 * share, channels), jnp.float32),
            pltpu.VMEM((channels * rows, keys), jnp.float32),
            pltpu.VMEM((share * height, keys), jnp.float32),
            pltpu.VMEM((share * height, keys), jnp.float32),
        ],
        compiler_params=pltpu.CompilerParams(vmem_limit_bytes=CLAIM * MIB),
        cost_estimate=pl.CostEstimate(
            flops=8 * share * channels * height * keys,
            bytes_accessed=2 * pair_in.size,
            transcendentals=0,
        ),
        name="pair_project",
    )(me, pair_in, tri_weight)


def pair_update_kernel(came, own, gate_w, out_w, bias_w, *refs):
    back, bias0, bias1, rows_a, rows_b, rows_c = refs[-6:]
    channels, count, keys = came.shape
    over_rows = (((0,), (0,)), ((), ()))

    def by_channel(value, rows):
        rows[...] = value.astype(jnp.float32).reshape(channels * count, keys)
        return jnp.concatenate([rows[pl.ds(u, channels, stride=count), :] for u in range(count)], 1)

    def normed(value):
        return channel_norm(value, 0).astype(jnp.bfloat16)

    pair = by_channel(own[...], rows_a)
    sums = by_channel(came[...], rows_b)
    gate = lax.dot_general(gate_w[0], normed(pair), over_rows, preferred_element_type=jnp.float32)
    update = lax.dot_general(out_w[...], normed(sums), over_rows, preferred_element_type=jnp.float32)
    new = (pair + jax.nn.sigmoid(gate) * update).astype(jnp.bfloat16).astype(jnp.float32)
    bias = jnp.dot(bias_w[...], normed(new), preferred_element_type=jnp.float32)
    for u in range(count):
        at = slice(u * keys, (u + 1) * keys)
        rows_b[pl.ds(u, channels, stride=count), :] = new[:, at]
        rows_c[pl.ds(u, bias.shape[0], stride=count), :] = bias[:, at]
    back[...] = rows_b[...].reshape(channels, count, keys).astype(jnp.bfloat16)
    both = rows_c[...].reshape((2,) + bias0.shape[1:]).astype(jnp.bfloat16)
    for k in range(bias0.shape[0]):
        bias0[k] = both[0]
        bias1[k] = both[1]


def pair_update(came, own, tri_weight, out_weight, bias_w, samp_size, col_size, others):
    channels, count, keys = came.shape
    heads = bias_w.shape[0] // 2
    message = jax.ShapeDtypeStruct(
        (samp_size, col_size, heads // col_size, count, keys), jnp.bfloat16
    )
    return local_call(
        pair_update_kernel,
        (jax.ShapeDtypeStruct(came.shape, jnp.bfloat16), message, message),
        [
            whole(came.shape),
            whole(own.shape),
            layer_block(tri_weight.shape, 0, 4),
            whole(out_weight.shape),
            whole(bias_w.shape),
        ]
        + [UNREAD] * len(others),
        [came, own, tri_weight, out_weight, bias_w, *others],
        [
            pltpu.VMEM((channels * count, keys), jnp.float32),
            pltpu.VMEM((channels * count, keys), jnp.float32),
            pltpu.VMEM((bias_w.shape[0] * count, keys), jnp.float32),
        ],
        6 * channels * channels * count * keys,
        "pair_update",
    )


def pair_rows_kernel(came, out):
    for c in range(came.shape[1]):
        rows = [came[k, c].astype(jnp.float32) for k in range(came.shape[0])]
        out[c] = jnp.concatenate(rows, 0).astype(jnp.bfloat16)


def pair_rows_joined(came):
    parts, share, count, keys = came.shape
    return local_call(
        pair_rows_kernel,
        jax.ShapeDtypeStruct((share, parts * count, keys), jnp.bfloat16),
        [whole(came.shape)],
        [came],
        [],
        0,
        "pair_rows",
    )


def body(
    pair_in,
    token_act,
    single,
    noise_sigma,
    token_mask,
    tri_weight,
    out_weight,
    bias_weight,
    time_weight,
    mod_weight,
    query_weight,
    key_weight,
    value_gate_weight,
    attn_out_weight,
    up_weight,
    down_weight,
):
    channels, pair_rows, pair_cols = pair_in.shape
    samp_size, row_size, col_size = (lax.axis_size(name) for name in ("samp", "row", "col"))
    group = row_size * col_size
    share = channels // samp_size
    halves = group // share
    half_rows = pair_rows // halves
    cell_rows = half_rows // samp_size
    own_rows = halves * cell_rows
    samp_at = jnp.reshape(lax.axis_index("samp"), (1,))
    row_at = jnp.reshape(lax.axis_index("row"), (1,))
    col_at = jnp.reshape(lax.axis_index("col"), (1,))
    blocks, _, head_count = bias_weight.shape

    state = jnp.swapaxes(token_act, 1, 2).astype(jnp.float32)
    samples, width, row_count = state.shape
    query_w = jnp.swapaxes(query_weight, 1, 2)
    key_w = jnp.swapaxes(key_weight, 1, 2)
    value_gate_w = jnp.swapaxes(value_gate_weight, 2, 3)
    mod_w = jnp.swapaxes(mod_weight, 2, 3)
    out_w = attn_out_weight.reshape(blocks, width, col_size, width)
    out_w = lax.all_to_all(jnp.transpose(out_w, (2, 0, 1, 3)), "col", 0, 0, tiled=True)
    half_count = TEMB // 2
    frequency = jnp.exp(jnp.arange(half_count, dtype=jnp.float32) * (math.log(100.0) / half_count))
    angles = (jnp.log(noise_sigma) * 0.25)[:, None] * frequency[None, :]
    time_embed = jnp.concatenate([jnp.cos(angles), jnp.sin(angles)], 1).astype(jnp.bfloat16)
    time_shift = jnp.dot(time_embed, time_weight, preferred_element_type=jnp.float32)
    mods, shared = modulate(single, time_shift, mod_w)
    shared = lax.all_gather(shared, "col", axis=0)
    mask_row = token_mask.astype(jnp.bfloat16)[None]

    sums = jnp.stack([jnp.sum(state, 1), jnp.sum(state * state, 1)])
    sums = sum(swap_all(sums, "col"))
    mean_value = sums[0] / DA
    scale = lax.rsqrt(sums[1] / DA - mean_value * mean_value + EPS)
    normed = (state - mean_value[:, None, :]) * scale[:, None, :]
    attn_local = (mods[0] * normed + mods[1]).astype(jnp.bfloat16)
    trans_local = (mods[2] * normed + mods[3]).astype(jnp.bfloat16)
    attn_full = lax.all_gather(attn_local, "col", axis=0)
    queries, gates, both = project([attn_full], query_w, key_w, value_gate_w, mask_row, 0)
    pieces = swap_all(both, "row")
    trans_full = lax.all_gather(trans_local, "col", axis=0)
    own, parts = transition([trans_full], col_at, up_weight, down_weight, 0, col_size)
    trans_came = [swap(parts[k - 1], "col", k) for k in range(1, col_size)]

    to_send = pair_project(pair_in, tri_weight, samp_at, group, samp_size)
    came = lax.all_to_all(to_send, ("row", "col"), 0, 0, tiled=True)
    came = came.reshape(row_size, col_size, half_rows + pair_rows, pair_cols)
    triangle = triangle_sums(came, [attn_full, out_w])
    triangle = triangle.reshape(samp_size * group, cell_rows, pair_cols)
    triangle = lax.all_to_all(triangle, ("samp", "row", "col"), 0, 0, tiled=True)
    triangle = triangle.reshape(channels, own_rows, pair_cols)

    own_pair = lax.dynamic_slice_in_dim(pair_in, samp_at[0] * own_rows, own_rows, 1)
    bias_w = jnp.swapaxes(bias_weight, 1, 2).reshape(blocks * head_count, channels)
    pair_out, *biases = pair_update(
        triangle, own_pair, tri_weight, out_weight, bias_w, samp_size, col_size, [both, own]
    )

    def spread_bias(part):
        shape = part.shape
        part = part.reshape((samp_size * col_size,) + shape[2:])
        return lax.all_to_all(part, ("samp", "col"), 0, 0, tiled=True).reshape(shape)

    biases = [spread_bias(part) for part in biases]

    for layer in range(blocks):
        if layer > 0:
            queries, gates, both = project(
                [state, shared], query_w, key_w, value_gate_w, mask_row, layer
            )
            own, parts = transition([state, shared], col_at, up_weight, down_weight, layer, col_size)
            pieces = swap_all(both, "row")
            trans_came = [swap(parts[k - 1], "col", k) for k in range(1, col_size)]
            pair_back = lax.all_to_all(
                after(pair_out, [both]).reshape(samp_size, share, own_rows, pair_cols),
                "samp",
                0,
                0,
                tiled=True,
            )
            pair_back = pair_rows_joined(pair_back)
        attended = attention(
            row_at, queries, gates, pieces, biases[layer], [pair_back] if layer > 0 else []
        )
        attended = lax.all_gather(attended, "col", axis=0)
        state = finish(
            attended, out_w, own, trans_came, mods, layer, 4 + 2 * layer, jnp.bfloat16
        )
        if layer < blocks - 1:
            state = lax.all_gather(state, "col", axis=0)
    return (pair_back, jnp.swapaxes(state, 1, 2))


def solution(mesh):
    placed = (
        P(None, "row", "col"),
        P("samp", "row", "col"),
        P("row", None),
        P("samp"),
        P("row"),
        P(),
        P(),
        P(),
        P(),
        P(None, None, None, "col"),
        P(None, None, "col"),
        P(None, None, "col"),
        P(None, None, None, "col"),
        P(None, "col", None),
        P(None, None, None, "col"),
        P(None, "col", None),
    )
    return jax.shard_map(
        body,
        mesh=mesh,
        in_specs=placed,
        out_specs=(P("samp", "row", "col"), P("samp", "row", "col")),
        check_vma=False,
    )
```

```python
import math

import jax
import jax.numpy as jnp
from jax import lax
from jax.experimental import pallas as pl
from jax.experimental.pallas import tpu as pltpu
from jax.sharding import PartitionSpec as P

DA = 768
HEAD_DIM = 48
TEMB = 256


EPS = 1e-05
MASK_FILL = 1000000000.0
MIB = 1024 * 1024
CLAIM = 63
MASK_ROWS = 16
NEAR = 4


def channel_norm(values, axis):
    mean_value = jnp.mean(values, axis=axis, keepdims=True)
    centred = values - mean_value
    spread = jnp.mean(centred * centred, axis=axis, keepdims=True)
    return centred * lax.rsqrt(spread + EPS)


def swap(value, axis, flip):
    size = lax.axis_size(axis)
    return lax.ppermute(value, axis, [(k, k ^ flip) for k in range(size)])


def swap_all(value, axis):
    return [value] + [swap(value, axis, flip) for flip in range(1, lax.axis_size(axis))]


def expected(micros):
    return pl.CostEstimate(flops=0, bytes_accessed=int(micros * 3.69e6), transcendentals=0)


def local_call(kernel, out_shape, in_specs, args, scratch, micros, name):
    return pl.pallas_call(
        kernel,
        grid=(1,),
        out_shape=out_shape,
        in_specs=in_specs,
        out_specs=jax.tree.map(lambda o: whole(o.shape), out_shape),
        scratch_shapes=scratch,
        compiler_params=pltpu.CompilerParams(vmem_limit_bytes=CLAIM * MIB),
        cost_estimate=expected(micros),
        name=name,
    )(*args)


def whole(shape):
    return pl.BlockSpec(tuple(shape), lambda i: (0,) * len(shape))


def layer_block(shape, at, layer):
    block = tuple(1 if d == at else n for d, n in enumerate(shape))
    return pl.BlockSpec(block, lambda i: tuple(layer if d == at else 0 for d in range(len(shape))))


SCALAR = pl.BlockSpec(memory_space=pltpu.SMEM)
UNREAD = pl.BlockSpec(memory_space=pl.ANY)


def after(value, others):
    return pl.pallas_call(
        lambda *refs: None,
        out_shape=jax.ShapeDtypeStruct(value.shape, value.dtype),
        in_specs=[UNREAD] * (1 + len(others)),
        out_specs=UNREAD,
        input_output_aliases={0: 0},
        name="after",
    )(value, *others)


def stack_gathered(gathered, full):
    parts, samples, width, tokens = gathered.shape
    for k in range(parts):
        for s in range(samples):
            full[k * width : (k + 1) * width, s * tokens : (s + 1) * tokens] = gathered[k, s]


def stack_normed(gathered, shared, full, normed):
    parts, samples, width, tokens = gathered.shape
    for s in range(samples):
        at = slice(s * tokens, (s + 1) * tokens)
        value = jnp.concatenate([gathered[k, s] for k in range(parts)], 0).astype(jnp.float32)
        value = channel_norm(value, 0)
        normed[:, at] = value
        for k in range(parts):
            gain, shift = shared[k, 0, s], shared[k, 1, s]
            full[k * width : (k + 1) * width, at] = (
                gain.astype(jnp.float32) * value[k * width : (k + 1) * width]
                + shift.astype(jnp.float32)
            ).astype(jnp.bfloat16)


def project_full(full, query_w, key_w, value_gate_w, mask, queries, gates, both):
    samples, width, tokens = queries.shape

    def times(weight):
        return jnp.dot(weight, full[...], preferred_element_type=jnp.float32).astype(jnp.bfloat16)

    key, value = times(key_w[0]), times(value_gate_w[0, 0])
    query, gate = times(query_w[0]), times(value_gate_w[0, 1])
    for s in range(samples):
        at = slice(s * tokens, (s + 1) * tokens)
        queries[s] = query[:, at]
        gates[s] = gate[:, at]
        both[2 * s * width : (2 * s + 1) * width] = key[:, at]
        both[(2 * s + 1) * width : (2 * s + 2) * width] = value[:, at]
    both[2 * samples * width :] = jnp.broadcast_to(mask[...], (MASK_ROWS, tokens))


def project_kernel(gathered, *refs):
    stack_gathered(gathered, refs[-1])
    project_full(refs[-1], *refs[:-1])


def normed_project_kernel(me_ref, gathered, shared, gain, shift, *refs):
    query_w, key_w, value_gate_w, mask, queries, gates, both, trans, full, normed = refs
    stack_normed(gathered, shared, full, normed)
    samples, width, tokens = trans.shape
    start = pl.multiple_of(me_ref[0] * width, width)
    for s in range(samples):
        piece = normed[pl.ds(start, width), s * tokens : (s + 1) * tokens]
        trans[s] = (gain[0, s] * piece + shift[0, s]).astype(jnp.bfloat16)
    project_full(full, query_w, key_w, value_gate_w, mask, queries, gates, both)


def mod_block(mods, m):
    return pl.BlockSpec((1,) + mods.shape[1:], lambda i: (m, 0, 0, 0))


def project(blocks, query_w, key_w, value_gate_w, mask, layer, me=None, shared=None, mods=None):
    samples, width, tokens = blocks[0].shape[-3:]
    small = jax.ShapeDtypeStruct((samples, width, tokens), jnp.bfloat16)
    joint = jax.ShapeDtypeStruct((2 * samples * width + MASK_ROWS, tokens), jnp.bfloat16)
    depth = query_w.shape[2]
    specs = [
        layer_block(query_w.shape, 0, layer),
        layer_block(key_w.shape, 0, layer),
        layer_block(value_gate_w.shape, 0, layer),
        whole(mask.shape),
    ]
    args = [query_w, key_w, value_gate_w, mask]
    full = pltpu.VMEM((depth, samples * tokens), jnp.bfloat16)
    if shared is None:
        return local_call(
            project_kernel,
            (small, small, joint),
            [whole(blocks[0].shape)] + specs,
            [*blocks, *args],
            [full],
            3.0,
            "project",
        )
    specs = [whole(blocks[0].shape), whole(shared.shape), mod_block(mods, 6), mod_block(mods, 7)] + specs
    return local_call(
        normed_project_kernel,
        (small, small, joint, small),
        [SCALAR] + specs,
        [me, *blocks, shared, mods, mods, *args],
        [full, pltpu.VMEM((depth, samples * tokens), jnp.float32)],
        4.0,
        "normed_project",
    )


def hand_out(total, me, keep, give):
    samples, width, tokens = keep.shape[1:]
    for e in range(keep.shape[0]):
        for target, flip in ((keep, 2 * e), (give, 2 * e + 1)):
            start = pl.multiple_of((me ^ flip) * width, width)
            for s in range(samples):
                piece = total[pl.ds(start, width), s * tokens : (s + 1) * tokens]
                target[e, s] = piece.astype(target.dtype)


def join_kernel(keep, came, out):
    out[...] = (keep[0] + came[0].astype(jnp.float32)).astype(out.dtype)


def sum_parts(keep, give):
    came = swap(give, "col", 1)
    far = local_call(
        join_kernel,
        jax.ShapeDtypeStruct(keep.shape[1:], jnp.bfloat16),
        [pl.BlockSpec((1,) + keep.shape[1:], lambda i: (1, 0, 0, 0))] * 2,
        [keep, came],
        [],
        1.0,
        "join",
    )
    return [keep, came, swap(far, "col", 2)]


def transition_kernel(me_ref, gathered, up, down, keep, give, full, total):
    stack_gathered(gathered, full)
    over_rows = (((0,), (0,)), ((), ()))
    swish = lax.dot_general(up[0, 0], full[...], over_rows, preferred_element_type=jnp.float32)
    linear = lax.dot_general(up[0, 1], full[...], over_rows, preferred_element_type=jnp.float32)
    hidden = (swish / (1.0 + jnp.exp(-swish)) * linear).astype(jnp.bfloat16)
    total[...] = lax.dot_general(down[0], hidden, over_rows, preferred_element_type=jnp.float32)
    hand_out(total, me_ref[0], keep, give)


def transition(gathered, me, up, down, layer, col_size):
    samples, width, tokens = gathered.shape[1:]
    depth, hidden = up.shape[2:]
    return local_call(
        transition_kernel,
        tuple(
            jax.ShapeDtypeStruct((col_size // 2, samples, width, tokens), dtype)
            for dtype in (jnp.float32, jnp.bfloat16)
        ),
        [SCALAR, whole(gathered.shape)]
        + [layer_block(up.shape, 0, layer), layer_block(down.shape, 0, layer)],
        [me, gathered, up, down],
        [
            pltpu.VMEM((depth, samples * tokens), jnp.bfloat16),
            pltpu.VMEM((depth, samples * tokens), jnp.float32),
        ],
        3.8,
        "transition",
    )


def attention_kernel(me_ref, queries, gates, kv0, kv1, kv2, kv3, bias0, bias1, bias2, bias3, *refs):
    out_w, keep, give, full, total, added = refs[0], *refs[-5:]
    pieces, biases = (kv0, kv1, kv2, kv3), (bias0, bias1, bias2, bias3)
    row_at, near_at, col_at = me_ref[0], me_ref[1], me_ref[2]
    samples, width, tokens = queries.shape
    far, cols, _, heads, count, keys = bias0.shape
    for k, bias in enumerate(biases):
        for z in range(far):
            start = pl.multiple_of((z * len(biases) + (near_at ^ k)) * count, count)
            for j in range(cols):
                added[:, pl.ds(start, count), j * keys : (j + 1) * keys] = bias[
                    z, row_at ^ j, 0
                ].astype(jnp.float32)
    scale = 1.0 / math.sqrt(HEAD_DIM)
    lane = lax.broadcasted_iota(jnp.int32, (tokens, width), 1) // HEAD_DIM
    masks = jnp.concatenate(
        [kv[2 * samples * width : 2 * samples * width + 1].astype(jnp.float32) for kv in pieces], 1
    )
    mask_add = (masks - 1.0) * MASK_FILL
    for s in range(samples):
        query = jnp.transpose(queries[s].astype(jnp.float32))
        key = jnp.concatenate([kv[2 * s * width : (2 * s + 1) * width] for kv in pieces], 1)
        value = jnp.concatenate([kv[(2 * s + 1) * width : (2 * s + 2) * width] for kv in pieces], 1)
        kept = jnp.zeros((tokens, width), jnp.float32)
        for h in range(heads):
            mine = lane == h
            scores = jnp.dot(
                jnp.where(mine, query, 0.0).astype(jnp.bfloat16),
                key,
                preferred_element_type=jnp.float32,
            )
            scores = scores * scale + added[h] + mask_add
            exps = jnp.exp(scores - jnp.max(scores, axis=1, keepdims=True))
            norm = jnp.sum(exps, axis=1, keepdims=True)
            product = lax.dot_general(
                exps.astype(jnp.bfloat16),
                value,
                (((1,), (1,)), ((), ())),
                preferred_element_type=jnp.float32,
            )
            kept = jnp.where(mine, product / norm, kept)
        gate = jax.nn.sigmoid(gates[s].astype(jnp.float32))
        full[:, s * tokens : (s + 1) * tokens] = (gate * jnp.transpose(kept)).astype(jnp.bfloat16)
    total[...] = lax.dot_general(
        out_w[0], full[...], (((0,), (0,)), ((), ())), preferred_element_type=jnp.float32
    )
    hand_out(total, col_at, keep, give)


def attention(me, queries, gates, pieces, biases, out_w, layer, others):
    samples, width, tokens = queries.shape
    heads = biases[0].shape[3]
    parts = out_w.shape[2] // width
    args = [me, queries, gates, *pieces]
    return local_call(
        attention_kernel,
        tuple(
            jax.ShapeDtypeStruct((parts // 2,) + queries.shape, dtype)
            for dtype in (jnp.float32, jnp.bfloat16)
        ),
        [SCALAR]
        + [whole(a.shape) for a in args[1:]]
        + [layer_block(b.shape, 2, layer) for b in biases]
        + [layer_block(out_w.shape, 0, layer)]
        + [UNREAD] * len(others),
        [*args, *biases, out_w, *others],
        [
            pltpu.VMEM((width, samples * tokens), jnp.bfloat16),
            pltpu.VMEM((parts * width, samples * tokens), jnp.float32),
            pltpu.VMEM((heads, tokens, len(pieces) * tokens), jnp.float32),
        ],
        5.4,
        "attention",
    )


def finish_kernel(keep_a, came_a, far_a, keep_t, came_t, far_t, gate_a, gate_t, *refs):
    state = refs[-1]
    for s in range(state.shape[0]):
        branch, trans = (
            keep[0, s] + came[0, s].astype(jnp.float32) + far[s].astype(jnp.float32)
            for keep, came, far in ((keep_a, came_a, far_a), (keep_t, came_t, far_t))
        )
        state[s] = (gate_a[0, s] * branch + gate_t[0, s] * trans).astype(state.dtype)


def finish(attended, trans, mods, gate_at, others):
    block = mods.shape[1:]
    first = pl.BlockSpec((1,) + block, lambda i: (0, 0, 0, 0))
    return local_call(
        finish_kernel,
        jax.ShapeDtypeStruct(block, jnp.bfloat16),
        [first, first, whole(block)] * 2
        + [mod_block(mods, gate_at), mod_block(mods, gate_at + 1)]
        + [UNREAD] * len(others),
        [*attended, *trans, mods, mods, *others],
        [],
        2.0,
        "finish",
    )


def modulate_kernel(single, shift, mod_w, *refs):
    own, shared, normed = refs[-3:]
    samples, width, tokens = own.shape[1:]
    layers, count = mod_w.shape[:2]
    for s in range(samples):
        condition = single[...].astype(jnp.float32) + shift[s : s + 1, :]
        normed[s * tokens : (s + 1) * tokens] = channel_norm(condition, 1).astype(jnp.bfloat16)
    kept = 0
    for layer in range(layers):
        for m in range(count):
            made = lax.dot_general(
                mod_w[layer, m],
                normed[...],
                (((1,), (1,)), ((), ())),
                preferred_element_type=jnp.float32,
            )
            if m not in (1, 3):
                made = jax.nn.sigmoid(made)
            for s in range(samples):
                piece = made[:, s * tokens : (s + 1) * tokens]
                if layer > 0 and m < 2:
                    shared[m, s] = piece.astype(jnp.bfloat16)
                else:
                    own[kept, s] = piece
            kept += layer == 0 or m >= 2


def modulate(single, shift, mod_w, others):
    layers, count, width, depth = mod_w.shape
    tokens, samples = single.shape[0], shift.shape[0]
    return local_call(
        modulate_kernel,
        (
            jax.ShapeDtypeStruct((count + 4, samples, width, tokens), jnp.float32),
            jax.ShapeDtypeStruct((2, samples, width, tokens), jnp.bfloat16),
        ),
        [whole(single.shape), whole(shift.shape), whole(mod_w.shape)] + [UNREAD] * len(others),
        [single, shift, mod_w, *others],
        [pltpu.VMEM((samples * tokens, depth), jnp.bfloat16)],
        4.8,
        "modulate",
    )


def first_inputs_kernel(state, sums, mods, attn, trans):
    mean_value = sums[0] / DA
    scale = lax.rsqrt(sums[1] / DA - mean_value * mean_value + EPS)
    for s in range(state.shape[0]):
        normed = (state[s].astype(jnp.float32) - mean_value[s : s + 1]) * scale[s : s + 1]
        attn[s] = (mods[0, s] * normed + mods[1, s]).astype(jnp.bfloat16)
        trans[s] = (mods[2, s] * normed + mods[3, s]).astype(jnp.bfloat16)


def first_inputs(state, sums, mods):
    out = jax.ShapeDtypeStruct(state.shape, jnp.bfloat16)
    return local_call(
        first_inputs_kernel,
        (out, out),
        [
            whole(state.shape),
            whole(sums.shape),
            pl.BlockSpec((4,) + state.shape, lambda i: (0, 0, 0, 0)),
        ],
        [state, sums, mods],
        [],
        2.0,
        "first_inputs",
    )


def triangle_kernel(came, *refs):
    out = refs[-1]
    rows, cols, _, keys = came.shape
    half = 8 * out.shape[0]

    def joined(at):
        return jnp.concatenate(
            [jnp.concatenate([came[r, c, at] for c in range(cols)], 1) for r in range(rows)], 0
        )

    sums = lax.dot_general(
        joined(slice(0, half)),
        joined(slice(half, half + keys)),
        (((1,), (1,)), ((), ())),
        preferred_element_type=jnp.float32,
    )
    groups = half // 8
    upper = lax.broadcasted_iota(jnp.int32, (groups, 8, keys), 1) < 4
    for r in range(rows):
        for c in range(0, cols, 2):
            one, two = (
                sums[r * half : (r + 1) * half, k * keys : (k + 1) * keys].reshape(groups, 8, keys)
                for k in (c, c + 1)
            )
            even = jnp.where(upper, one, pltpu.roll(two, 4, 1))
            odd = jnp.where(upper, pltpu.roll(one, 4, 1), two)
            out[:, 0, r, c // 2] = even.astype(jnp.bfloat16)
            out[:, 1, r, c // 2] = odd.astype(jnp.bfloat16)


def triangle_sums(came, others):
    rows, cols, height, keys = came.shape
    half = height - keys
    left = rows * half
    return local_call(
        triangle_kernel,
        jax.ShapeDtypeStruct((half // 8, 2, rows, cols // 2, 8, keys), jnp.bfloat16),
        [whole(came.shape)] + [UNREAD] * len(others),
        [came, *others],
        [],
        2.2,
        "triangle_sums",
    )


def pair_project_kernel(me_ref, pair, tri, *refs):
    out, weight, normed, left, right = refs[-5:]
    step = pl.program_id(0)
    channels, rows, keys = pair.shape
    height = rows * pl.num_programs(0)
    share = weight.shape[0] // 4
    halves = out.shape[0] // share
    part = out.shape[1] - keys
    group = 8 // halves

    @pl.when(step == 0)
    def _():
        mine = lax.broadcasted_iota(jnp.int32, (share, channels), 0) + me_ref[0] * share
        pick = mine == lax.broadcasted_iota(jnp.int32, (share, channels), 1)
        for p in range(4):
            weight[p * share : (p + 1) * share] = lax.dot_general(
                pick.astype(jnp.bfloat16),
                tri[p],
                (((1,), (1,)), ((), ())),
                preferred_element_type=jnp.float32,
            )

    value = pair[...].astype(jnp.float32)
    normed[...] = channel_norm(value, 0).reshape(channels * rows, keys)
    weights = weight[...].astype(jnp.bfloat16)
    for i in range(0, rows, 2):
        two = [normed[pl.ds(i + e, channels, stride=rows), :] for e in (0, 1)]
        made = jnp.dot(
            weights, jnp.concatenate(two, 1).astype(jnp.bfloat16), preferred_element_type=jnp.float32
        )
        made_left = jax.nn.sigmoid(made[:share]) * made[share : 2 * share]
        made_right = jax.nn.sigmoid(made[2 * share : 3 * share]) * made[3 * share :]
        for e in (0, 1):
            row, at = i + e, slice(e * keys, (e + 1) * keys)
            right[pl.ds(step * rows + row, share, stride=keys), :] = made_right[:, at]
            place = (row % 8) // group * part + row // 8 * group + row % group
            place = step * (rows // 8 * group) + place
            left[pl.ds(place, share, stride=keys), :] = made_left[:, at]

    @pl.when(step == pl.num_programs(0) - 1)
    def _():
        for c in range(share):
            whole_right = right[c * keys : (c + 1) * keys].astype(jnp.bfloat16)
            for h in range(halves):
                start = c * keys + h * part
                out[c * halves + h, :part] = left[start : start + part].astype(jnp.bfloat16)
                out[c * halves + h, part:] = whole_right


def pair_project(pair_in, tri_weight, me, group, samp_size, others):
    channels, height, keys = pair_in.shape
    share = channels // samp_size
    part = height // (group // share)
    rows = 16
    out = jax.ShapeDtypeStruct((group, part + height, keys), jnp.bfloat16)
    return pl.pallas_call(
        pair_project_kernel,
        grid=(height // rows,),
        out_shape=out,
        in_specs=[
            SCALAR,
            pl.BlockSpec((channels, rows, keys), lambda i: (0, i, 0)),
            whole(tri_weight.shape),
        ]
        + [UNREAD] * len(others),
        out_specs=whole(out.shape),
        scratch_shapes=[
            pltpu.VMEM((4 * share, channels), jnp.float32),
            pltpu.VMEM((channels * rows, keys), jnp.float32),
            pltpu.VMEM((share * height, keys), jnp.float32),
            pltpu.VMEM((share * height, keys), jnp.float32),
        ],
        compiler_params=pltpu.CompilerParams(vmem_limit_bytes=CLAIM * MIB),
        cost_estimate=expected(9.7),
        name="pair_project",
    )(me, pair_in, tri_weight, *others)


def pair_update_kernel(came, own, gate_w, out_w, bias_w, *refs):
    back, message, rows_a, rows_b, rows_c = refs[-5:]
    channels, count, keys = came.shape
    over_rows = (((0,), (0,)), ((), ()))

    def by_channel(value, rows):
        rows[...] = value.astype(jnp.float32).reshape(channels * count, keys)
        return jnp.concatenate([rows[pl.ds(u, channels, stride=count), :] for u in range(count)], 1)

    def normed(value):
        return channel_norm(value, 0).astype(jnp.bfloat16)

    pair = by_channel(own[...], rows_a)
    sums = by_channel(came[...], rows_b)
    gate = lax.dot_general(gate_w[0], normed(pair), over_rows, preferred_element_type=jnp.float32)
    update = lax.dot_general(out_w[...], normed(sums), over_rows, preferred_element_type=jnp.float32)
    new = (pair + jax.nn.sigmoid(gate) * update).astype(jnp.bfloat16).astype(jnp.float32)
    bias = jnp.dot(bias_w[...], normed(new), preferred_element_type=jnp.float32)
    for u in range(count):
        at = slice(u * keys, (u + 1) * keys)
        rows_b[pl.ds(u, channels, stride=count), :] = new[:, at]
        rows_c[pl.ds(u, bias.shape[0], stride=count), :] = bias[:, at]
    back[...] = rows_b[...].reshape(channels, count, keys).astype(jnp.bfloat16)
    _, cols, layers, heads = message.shape[:4]
    made = rows_c[...].reshape(layers, cols, heads, count, keys).astype(jnp.bfloat16)
    for k in range(message.shape[0]):
        for layer in range(layers):
            message[k, :, layer] = made[layer]


def pair_update(came, own, tri_weight, out_weight, bias_w, layers, samp_size, col_size, others):
    channels, count, keys = came.shape
    heads = bias_w.shape[0] // (layers * col_size)
    message = jax.ShapeDtypeStruct(
        (samp_size, col_size, layers, heads, count, keys), jnp.bfloat16
    )
    return local_call(
        pair_update_kernel,
        (jax.ShapeDtypeStruct(came.shape, jnp.bfloat16), message),
        [
            whole(came.shape),
            whole(own.shape),
            layer_block(tri_weight.shape, 0, 4),
            whole(out_weight.shape),
            whole(bias_w.shape),
        ]
        + [UNREAD] * len(others),
        [came, own, tri_weight, out_weight, bias_w, *others],
        [
            pltpu.VMEM((channels * count, keys), jnp.float32),
            pltpu.VMEM((channels * count, keys), jnp.float32),
            pltpu.VMEM((bias_w.shape[0] * count, keys), jnp.float32),
        ],
        2.8,
        "pair_update",
    )


def pair_rows_kernel(came, out):
    for c in range(came.shape[1]):
        rows = [came[k, c].astype(jnp.float32) for k in range(came.shape[0])]
        out[c] = jnp.concatenate(rows, 0).astype(jnp.bfloat16)


def pair_rows_joined(came):
    parts, share, count, keys = came.shape
    return local_call(
        pair_rows_kernel,
        jax.ShapeDtypeStruct((share, parts * count, keys), jnp.bfloat16),
        [whole(came.shape)],
        [came],
        [],
        1.7,
        "pair_rows",
    )


def body(
    pair_in,
    token_act,
    single,
    noise_sigma,
    token_mask,
    tri_weight,
    out_weight,
    bias_weight,
    time_weight,
    mod_weight,
    query_weight,
    key_weight,
    value_gate_weight,
    attn_out_weight,
    up_weight,
    down_weight,
):
    channels, pair_rows, pair_cols = pair_in.shape
    samp_size, row_size, col_size = (lax.axis_size(name) for name in ("samp", "row", "col"))
    group = row_size * col_size
    share = channels // samp_size
    halves = group // share
    half_rows = pair_rows // halves
    cell_rows = half_rows // samp_size
    own_rows = halves * cell_rows
    samp_at = jnp.reshape(lax.axis_index("samp"), (1,))
    row_at = jnp.reshape(lax.axis_index("row"), (1,))
    col_at = jnp.reshape(lax.axis_index("col"), (1,))
    blocks, _, head_count = bias_weight.shape

    state = jnp.swapaxes(token_act, 1, 2)
    samples, width, row_count = state.shape
    wide = state.astype(jnp.float32)
    sums = jnp.stack([jnp.sum(wide, 1), jnp.sum(wide * wide, 1)])
    sums = sum(swap_all(sums, "col"))
    query_w = jnp.swapaxes(query_weight, 1, 2)
    key_w = jnp.swapaxes(key_weight, 1, 2)
    value_gate_w = jnp.swapaxes(value_gate_weight, 2, 3)
    mod_w = jnp.swapaxes(mod_weight, 2, 3)
    half_count = TEMB // 2
    frequency = jnp.exp(jnp.arange(half_count, dtype=jnp.float32) * (math.log(100.0) / half_count))
    angles = (jnp.log(noise_sigma) * 0.25)[:, None] * frequency[None, :]
    time_embed = jnp.concatenate([jnp.cos(angles), jnp.sin(angles)], 1).astype(jnp.bfloat16)
    time_shift = jnp.dot(time_embed, time_weight, preferred_element_type=jnp.float32)

    to_send = pair_project(pair_in, tri_weight, samp_at, group, samp_size, [sums])
    came = lax.all_to_all(to_send, ("row", "col"), 0, 0, tiled=True)
    came = came.reshape(row_size, col_size, half_rows + pair_rows, pair_cols)

    mods, shared = modulate(single, time_shift, mod_w, [to_send])
    attn_local, trans_local = first_inputs(state, sums, mods)
    attn_full = lax.all_gather(attn_local, "col", axis=0)

    triangle = triangle_sums(came, [attn_full])
    shared = lax.all_gather(shared, "col", axis=0)
    triangle = triangle.reshape(samp_size * group, cell_rows, pair_cols)
    triangle = lax.all_to_all(triangle, ("samp", "row", "col"), 0, 0, tiled=True)
    triangle = triangle.reshape(channels, own_rows, pair_cols)
    mask_row = token_mask.astype(jnp.bfloat16)[None]
    queries, gates, both = project([attn_full], query_w, key_w, value_gate_w, mask_row, 0)
    pieces = swap_all(both, "row")

    own_pair = lax.dynamic_slice_in_dim(pair_in, samp_at[0] * own_rows, own_rows, 1)
    bias_w = jnp.swapaxes(bias_weight, 1, 2).reshape(blocks * head_count, channels)
    pair_out, bias = pair_update(
        triangle,
        own_pair,
        tri_weight,
        out_weight,
        bias_w,
        blocks,
        samp_size // NEAR,
        col_size,
        [both, shared],
    )
    far = samp_size // NEAR
    message = bias.shape
    bias = lax.all_to_all(
        bias.reshape((far * col_size,) + message[2:]),
        ("samp", "col"),
        0,
        0,
        axis_index_groups=[
            [(z * NEAR + x) * col_size + c for z in range(far) for c in range(col_size)]
            for x in range(NEAR)
        ],
        tiled=True,
    ).reshape(message)
    biases = [bias] + [
        lax.ppermute(bias, "samp", [(k, k ^ flip) for k in range(samp_size)])
        for flip in range(1, NEAR)
    ]
    pair_back = after(pair_out, [biases[1]]).reshape(samp_size, share, own_rows, pair_cols)
    pair_back = lax.all_to_all(pair_back, "samp", 0, 0, tiled=True)
    trans_full = lax.all_gather(trans_local, "col", axis=0)
    trans = transition(trans_full, col_at, up_weight, down_weight, 0, col_size)
    trans_sum = sum_parts(*trans)
    seat = jnp.concatenate([row_at, samp_at % NEAR, col_at])

    for layer in range(blocks):
        if layer > 0:
            queries, gates, both, trans_local = project(
                [state], query_w, key_w, value_gate_w, mask_row, layer, col_at, shared, mods
            )
            pieces = swap_all(both, "row")
            trans_full = lax.all_gather(trans_local, "col", axis=0)
            trans = transition(trans_full, col_at, up_weight, down_weight, layer, col_size)
            trans_sum = sum_parts(*trans)
        attended = attention(
            seat, queries, gates, pieces, biases, attn_out_weight, layer, [trans[0] if layer else trans_sum[2]]
        )
        state = finish(
            sum_parts(*attended), trans_sum, mods, 4 * (1 + layer), [] if layer else [pair_back]
        )
        if layer == 0:
            state = lax.all_gather(state, "col", axis=0)
    pair_back = pair_rows_joined(pair_back)
    return (pair_back, jnp.swapaxes(state, 1, 2))


def solution(mesh):
    placed = (
        P(None, "row", "col"),
        P("samp", "row", "col"),
        P("row", None),
        P("samp"),
        P("row"),
        P(),
        P(),
        P(),
        P(),
        P(None, None, None, "col"),
        P(None, None, "col"),
        P(None, None, "col"),
        P(None, None, None, "col"),
        P(None, "col", None),
        P(None, None, None, "col"),
        P(None, "col", None),
    )
    return jax.shard_map(
        body,
        mesh=mesh,
        in_specs=placed,
        out_specs=(P("samp", "row", "col"), P("samp", "row", "col")),
        check_vma=False,
    )
```

```python
import math

import jax
import jax.numpy as jnp
from jax import lax
from jax.experimental import pallas as pl
from jax.experimental.pallas import tpu as pltpu
from jax.sharding import PartitionSpec as P

DA = 768
HEAD_DIM = 48
TEMB = 256


EPS = 1e-05
MASK_FILL = 1000000000.0
MIB = 1024 * 1024
CLAIM = 63
MASK_ROWS = 16
NEAR = 4


def channel_norm(values, axis):
    mean_value = jnp.mean(values, axis=axis, keepdims=True)
    centred = values - mean_value
    spread = jnp.mean(centred * centred, axis=axis, keepdims=True)
    return centred * lax.rsqrt(spread + EPS)


def swap(value, axis, flip):
    size = lax.axis_size(axis)
    return lax.ppermute(value, axis, [(k, k ^ flip) for k in range(size)])


def swap_all(value, axis):
    return [value] + [swap(value, axis, flip) for flip in range(1, lax.axis_size(axis))]


def expected(micros):
    return pl.CostEstimate(flops=0, bytes_accessed=int(micros * 3.69e6), transcendentals=0)


def local_call(kernel, out_shape, in_specs, args, scratch, micros, name):
    return pl.pallas_call(
        kernel,
        grid=(1,),
        out_shape=out_shape,
        in_specs=in_specs,
        out_specs=jax.tree.map(lambda o: whole(o.shape), out_shape),
        scratch_shapes=scratch,
        compiler_params=pltpu.CompilerParams(vmem_limit_bytes=CLAIM * MIB),
        cost_estimate=expected(micros),
        name=name,
    )(*args)


def whole(shape):
    return pl.BlockSpec(tuple(shape), lambda i: (0,) * len(shape))


def layer_block(shape, at, layer):
    block = tuple(1 if d == at else n for d, n in enumerate(shape))
    return pl.BlockSpec(block, lambda i: tuple(layer if d == at else 0 for d in range(len(shape))))


SCALAR = pl.BlockSpec(memory_space=pltpu.SMEM)
UNREAD = pl.BlockSpec(memory_space=pl.ANY)


def after(value, others):
    return pl.pallas_call(
        lambda *refs: None,
        out_shape=jax.ShapeDtypeStruct(value.shape, value.dtype),
        in_specs=[UNREAD] * (1 + len(others)),
        out_specs=UNREAD,
        input_output_aliases={0: 0},
        name="after",
    )(value, *others)


def stack_gathered(gathered, full):
    parts, samples, width, tokens = gathered.shape
    for k in range(parts):
        for s in range(samples):
            full[k * width : (k + 1) * width, s * tokens : (s + 1) * tokens] = gathered[k, s]


def stack_normed(me, gathered, shared, own, full, normed, trans):
    parts, samples, width, tokens = gathered.shape
    for s in range(samples):
        at = slice(s * tokens, (s + 1) * tokens)
        value = jnp.concatenate([gathered[k, s] for k in range(parts)], 0).astype(jnp.float32)
        normed[...] = channel_norm(value, 0)
        for k, pair in enumerate(shared):
            rows = pl.ds(pl.multiple_of((me ^ k) * width, width), width)
            value = normed[rows, :]
            gain, shift = pair[0, s].astype(jnp.float32), pair[1, s].astype(jnp.float32)
            full[rows, at] = (gain * value + shift).astype(jnp.bfloat16)
            if k == 0:
                gain, shift = own[0, s].astype(jnp.float32), own[1, s].astype(jnp.float32)
                trans[s] = (gain * value + shift).astype(jnp.bfloat16)


def first_project_kernel(me_ref, block0, block1, block2, block3, *refs):
    stack_features((block0, block1, block2, block3), refs[-1], me_ref[0])
    project_full(*refs)


def later_project_kernel(me_ref, gathered, pair0, pair1, pair2, pair3, own, *refs):
    *rest, trans, full, normed = refs
    shared = (pair0, pair1, pair2, pair3)
    stack_normed(me_ref[0], gathered, shared, own, full, normed, trans)
    project_full(*rest, full)


def project_full(query_w, key_w, value_gate_w, mask, queries, gates, both, full):
    samples, width, tokens = queries.shape

    def times(weight):
        return jnp.dot(weight, full[...], preferred_element_type=jnp.float32).astype(jnp.bfloat16)

    key, value = times(key_w[0]), times(value_gate_w[0, 0])
    query, gate = times(query_w[0]), times(value_gate_w[0, 1])
    for s in range(samples):
        at = slice(s * tokens, (s + 1) * tokens)
        queries[s] = query[:, at]
        gates[s] = gate[:, at]
        both[2 * s * width : (2 * s + 1) * width] = key[:, at]
        both[(2 * s + 1) * width : (2 * s + 2) * width] = value[:, at]
    both[2 * samples * width :] = jnp.broadcast_to(
        mask[...].astype(jnp.float32), (MASK_ROWS, tokens)
    ).astype(jnp.bfloat16)


def project(blocks, me, query_w, key_w, value_gate_w, mask, layer, shared=None, own=None):
    samples, width, tokens = blocks[0].shape[-3:]
    small = jax.ShapeDtypeStruct((samples, width, tokens), jnp.bfloat16)
    joint = jax.ShapeDtypeStruct((2 * samples * width + MASK_ROWS, tokens), jnp.bfloat16)
    specs = [
        layer_block(query_w.shape, 0, layer),
        layer_block(key_w.shape, 0, layer),
        layer_block(value_gate_w.shape, 0, layer),
        whole(mask.shape),
    ]
    args = [query_w, key_w, value_gate_w, mask]
    depth = query_w.shape[2]
    full = pltpu.VMEM((depth, samples * tokens), jnp.bfloat16)
    if shared is None:
        return local_call(
            first_project_kernel,
            (small, small, joint),
            [SCALAR] + [whole(b.shape) for b in blocks] + specs,
            [me, *blocks, *args],
            [full],
            3.0,
            "first_project",
        )
    return local_call(
        later_project_kernel,
        (small, small, joint, small),
        [SCALAR] + [whole(a.shape) for a in (*blocks, *shared, own)] + specs,
        [me, *blocks, *shared, own, *args],
        [full, pltpu.VMEM((depth, tokens), jnp.float32)],
        4.0,
        "later_project",
    )


def mod_block(mods, m):
    return pl.BlockSpec((1,) + mods.shape[1:], lambda i: (m, 0, 0, 0))


def hand_out(total, me, keep, give):
    samples, width, tokens = keep.shape[1:]
    for e in range(keep.shape[0]):
        for target, flip in ((keep, 2 * e), (give, 2 * e + 1)):
            start = pl.multiple_of((me ^ flip) * width, width)
            for s in range(samples):
                piece = total[pl.ds(start, width), s * tokens : (s + 1) * tokens]
                target[e, s] = piece.astype(target.dtype)


def join_kernel(keep, came, out):
    out[...] = (keep[0] + came[0].astype(jnp.float32)).astype(out.dtype)


def sum_parts(keep, give):
    came = swap(give, "col", 1)
    far = local_call(
        join_kernel,
        jax.ShapeDtypeStruct(keep.shape[1:], jnp.bfloat16),
        [pl.BlockSpec((1,) + keep.shape[1:], lambda i: (1, 0, 0, 0))] * 2,
        [keep, came],
        [],
        1.0,
        "join",
    )
    return [keep, came, swap(far, "col", 2)], far


def stack_features(blocks, full, me):
    for k, block in enumerate(blocks):
        samples, width, tokens = block.shape
        start = pl.multiple_of((me ^ k) * width, width)
        for s in range(samples):
            full[pl.ds(start, width), s * tokens : (s + 1) * tokens] = block[s]


def transition_kernel(count, me_ref, *refs):
    up, down, keep, give, full, total = refs[count:]
    if count > 1:
        stack_features(refs[:count], full, me_ref[0])
    else:
        stack_gathered(refs[0], full)
    over_rows = (((0,), (0,)), ((), ()))
    swish = lax.dot_general(up[0, 0], full[...], over_rows, preferred_element_type=jnp.float32)
    linear = lax.dot_general(up[0, 1], full[...], over_rows, preferred_element_type=jnp.float32)
    hidden = (swish / (1.0 + jnp.exp(-swish)) * linear).astype(jnp.bfloat16)
    total[...] = lax.dot_general(down[0], hidden, over_rows, preferred_element_type=jnp.float32)
    hand_out(total, me_ref[0], keep, give)


def transition(blocks, me, up, down, layer, col_size):
    samples, width, tokens = blocks[0].shape[-3:]
    depth, hidden = up.shape[2:]
    return local_call(
        lambda *refs: transition_kernel(len(blocks), *refs),
        tuple(
            jax.ShapeDtypeStruct((col_size // 2, samples, width, tokens), dtype)
            for dtype in (jnp.float32, jnp.bfloat16)
        ),
        [SCALAR]
        + [whole(b.shape) for b in blocks]
        + [layer_block(up.shape, 0, layer), layer_block(down.shape, 0, layer)],
        [me, *blocks, up, down],
        [
            pltpu.VMEM((depth, samples * tokens), jnp.bfloat16),
            pltpu.VMEM((depth, samples * tokens), jnp.float32),
        ],
        3.8,
        "transition",
    )


def attention_kernel(me_ref, queries, gates, kv0, kv1, kv2, kv3, bias0, bias1, bias2, bias3, *refs):
    out_w, keep, give, full, total, added = refs[0], *refs[-5:]
    pieces, biases = (kv0, kv1, kv2, kv3), (bias0, bias1, bias2, bias3)
    row_at, near_at, col_at = me_ref[0], me_ref[1], me_ref[2]
    samples, width, tokens = queries.shape
    far, cols, _, heads, count, keys = bias0.shape
    for k, bias in enumerate(biases):
        for z in range(far):
            start = pl.multiple_of((z * len(biases) + (near_at ^ k)) * count, count)
            for j in range(cols):
                added[:, pl.ds(start, count), j * keys : (j + 1) * keys] = bias[
                    z, row_at ^ j, 0
                ].astype(jnp.float32)
    scale = 1.0 / math.sqrt(HEAD_DIM)
    lane = lax.broadcasted_iota(jnp.int32, (tokens, width), 1) // HEAD_DIM
    masks = jnp.concatenate(
        [kv[2 * samples * width : 2 * samples * width + 1].astype(jnp.float32) for kv in pieces], 1
    )
    mask_add = (masks - 1.0) * MASK_FILL
    for s in range(samples):
        query = jnp.transpose(queries[s].astype(jnp.float32))
        key = jnp.concatenate([kv[2 * s * width : (2 * s + 1) * width] for kv in pieces], 1)
        value = jnp.concatenate([kv[(2 * s + 1) * width : (2 * s + 2) * width] for kv in pieces], 1)
        kept = jnp.zeros((tokens, width), jnp.float32)
        for h in range(heads):
            mine = lane == h
            scores = jnp.dot(
                jnp.where(mine, query, 0.0).astype(jnp.bfloat16),
                key,
                preferred_element_type=jnp.float32,
            )
            scores = scores * scale + added[h] + mask_add
            exps = jnp.exp(scores - jnp.max(scores, axis=1, keepdims=True))
            norm = jnp.sum(exps, axis=1, keepdims=True)
            product = lax.dot_general(
                exps.astype(jnp.bfloat16),
                value,
                (((1,), (1,)), ((), ())),
                preferred_element_type=jnp.float32,
            )
            kept = jnp.where(mine, product / norm, kept)
        gate = jax.nn.sigmoid(gates[s].astype(jnp.float32))
        full[:, s * tokens : (s + 1) * tokens] = (gate * jnp.transpose(kept)).astype(jnp.bfloat16)
    total[...] = lax.dot_general(
        out_w[0], full[...], (((0,), (0,)), ((), ())), preferred_element_type=jnp.float32
    )
    hand_out(total, col_at, keep, give)


def attention(me, queries, gates, pieces, biases, out_w, layer, others):
    samples, width, tokens = queries.shape
    heads = biases[0].shape[3]
    parts = out_w.shape[2] // width
    args = [me, queries, gates, *pieces]
    return local_call(
        attention_kernel,
        tuple(
            jax.ShapeDtypeStruct((parts // 2,) + queries.shape, dtype)
            for dtype in (jnp.float32, jnp.bfloat16)
        ),
        [SCALAR]
        + [whole(a.shape) for a in args[1:]]
        + [layer_block(b.shape, 2, layer) for b in biases]
        + [layer_block(out_w.shape, 0, layer)]
        + [UNREAD] * len(others),
        [*args, *biases, out_w, *others],
        [
            pltpu.VMEM((width, samples * tokens), jnp.bfloat16),
            pltpu.VMEM((parts * width, samples * tokens), jnp.float32),
            pltpu.VMEM((heads, tokens, len(pieces) * tokens), jnp.float32),
        ],
        5.4,
        "attention",
    )


def finish_kernel(keep_a, came_a, far_a, keep_t, came_t, far_t, gate_a, gate_t, *refs):
    state = refs[-1]
    for s in range(state.shape[0]):
        branch, trans = (
            keep[0, s] + came[0, s].astype(jnp.float32) + far[s].astype(jnp.float32)
            for keep, came, far in ((keep_a, came_a, far_a), (keep_t, came_t, far_t))
        )
        value = gate_a[0, s].astype(jnp.float32) * branch + gate_t[0, s].astype(jnp.float32) * trans
        state[s] = value.astype(state.dtype)


def finish(attended, trans, mods, gate_at, others):
    block = mods.shape[1:]
    first = pl.BlockSpec((1,) + block, lambda i: (0, 0, 0, 0))
    return local_call(
        finish_kernel,
        jax.ShapeDtypeStruct(block, jnp.bfloat16),
        [first, first, whole(block)] * 2
        + [mod_block(mods, gate_at), mod_block(mods, gate_at + 1)]
        + [UNREAD] * len(others),
        [*attended, *trans, mods, mods, *others],
        [],
        2.0,
        "finish",
    )


def modulate_kernel(single, time_embed, time_w, mod_w, state, sums, *refs):
    attn, trans, gates, later, shared, normed = refs[-6:]
    samples, width, tokens = state.shape
    layers, count = mod_w.shape[:2]
    shift = jnp.dot(time_embed[...], time_w[...], preferred_element_type=jnp.float32)
    for s in range(samples):
        condition = single[...].astype(jnp.float32) + shift[s : s + 1, :]
        normed[s * tokens : (s + 1) * tokens] = channel_norm(condition, 1).astype(jnp.bfloat16)

    def made(layer, m):
        value = lax.dot_general(
            mod_w[layer, m],
            normed[...],
            (((1,), (1,)), ((), ())),
            preferred_element_type=jnp.float32,
        )
        value = value if m in (1, 3) else jax.nn.sigmoid(value)
        return [value[:, s * tokens : (s + 1) * tokens] for s in range(samples)]

    mean_value = sums[0] / DA
    scale = lax.rsqrt(sums[1] / DA - mean_value * mean_value + EPS)
    for target, m in ((attn, 0), (trans, 2)):
        gain, shift = made(0, m), made(0, m + 1)
        for s in range(samples):
            value = (state[s].astype(jnp.float32) - mean_value[s : s + 1]) * scale[s : s + 1]
            target[s] = (gain[s] * value + shift[s]).astype(jnp.bfloat16)
    for layer in range(layers):
        for m in range(4, count):
            for s, value in enumerate(made(layer, m)):
                gates[layer * (count - 4) + m - 4, s] = value.astype(jnp.bfloat16)
    for m in range(4):
        for s, value in enumerate(made(layers - 1, m)):
            target = shared if m < 2 else later
            target[m % 2, s] = value.astype(jnp.bfloat16)


def modulate(single, time_embed, time_w, mod_w, state, sums, others):
    layers, count, _, depth = mod_w.shape
    samples, _, tokens = state.shape
    args = [single, time_embed, time_w, mod_w, state, sums]
    return local_call(
        modulate_kernel,
        tuple(
            jax.ShapeDtypeStruct(lead + state.shape, jnp.bfloat16)
            for lead in ((), (), (2 * layers,), (2,), (2,))
        ),
        [whole(a.shape) for a in args] + [UNREAD] * len(others),
        args + others,
        [pltpu.VMEM((samples * tokens, depth), jnp.bfloat16)],
        4.5,
        "modulate",
    )


def triangle_kernel(came, *refs):
    out = refs[-1]
    rows, cols, _, keys = came.shape
    half = 8 * out.shape[0]

    def joined(at):
        return jnp.concatenate(
            [jnp.concatenate([came[r, c, at] for c in range(cols)], 1) for r in range(rows)], 0
        )

    sums = lax.dot_general(
        joined(slice(0, half)),
        joined(slice(half, half + keys)),
        (((1,), (1,)), ((), ())),
        preferred_element_type=jnp.float32,
    )
    groups = half // 8
    upper = lax.broadcasted_iota(jnp.int32, (groups, 8, keys), 1) < 4
    for r in range(rows):
        for c in range(0, cols, 2):
            one, two = (
                sums[r * half : (r + 1) * half, k * keys : (k + 1) * keys].reshape(groups, 8, keys)
                for k in (c, c + 1)
            )
            even = jnp.where(upper, one, pltpu.roll(two, 4, 1))
            odd = jnp.where(upper, pltpu.roll(one, 4, 1), two)
            out[:, 0, r, c // 2] = even.astype(jnp.bfloat16)
            out[:, 1, r, c // 2] = odd.astype(jnp.bfloat16)


def triangle_sums(came, others):
    rows, cols, height, keys = came.shape
    half = height - keys
    left = rows * half
    return local_call(
        triangle_kernel,
        jax.ShapeDtypeStruct((half // 8, 2, rows, cols // 2, 8, keys), jnp.bfloat16),
        [whole(came.shape)] + [UNREAD] * len(others),
        [came, *others],
        [],
        2.2,
        "triangle_sums",
    )


def pair_project_kernel(me_ref, pair, tri, *refs):
    out, weight, normed, left, right = refs[-5:]
    step = pl.program_id(0)
    channels, rows, keys = pair.shape
    height = rows * pl.num_programs(0)
    share = weight.shape[0] // 4
    halves = out.shape[0] // share
    part = out.shape[1] - keys
    group = 8 // halves

    @pl.when(step == 0)
    def _():
        mine = lax.broadcasted_iota(jnp.int32, (share, channels), 0) + me_ref[0] * share
        pick = mine == lax.broadcasted_iota(jnp.int32, (share, channels), 1)
        for p in range(4):
            weight[p * share : (p + 1) * share] = lax.dot_general(
                pick.astype(jnp.bfloat16),
                tri[p],
                (((1,), (1,)), ((), ())),
                preferred_element_type=jnp.float32,
            )

    value = pair[...].astype(jnp.float32)
    normed[...] = channel_norm(value, 0).reshape(channels * rows, keys)
    weights = weight[...].astype(jnp.bfloat16)
    for i in range(0, rows, 2):
        two = [normed[pl.ds(i + e, channels, stride=rows), :] for e in (0, 1)]
        made = jnp.dot(
            weights, jnp.concatenate(two, 1).astype(jnp.bfloat16), preferred_element_type=jnp.float32
        )
        made_left = jax.nn.sigmoid(made[:share]) * made[share : 2 * share]
        made_right = jax.nn.sigmoid(made[2 * share : 3 * share]) * made[3 * share :]
        for e in (0, 1):
            row, at = i + e, slice(e * keys, (e + 1) * keys)
            right[pl.ds(step * rows + row, share, stride=keys), :] = made_right[:, at]
            place = (row % 8) // group * part + row // 8 * group + row % group
            place = step * (rows // 8 * group) + place
            left[pl.ds(place, share, stride=keys), :] = made_left[:, at]

    @pl.when(step == pl.num_programs(0) - 1)
    def _():
        for c in range(share):
            whole_right = right[c * keys : (c + 1) * keys].astype(jnp.bfloat16)
            for h in range(halves):
                start = c * keys + h * part
                out[c * halves + h, :part] = left[start : start + part].astype(jnp.bfloat16)
                out[c * halves + h, part:] = whole_right


def pair_project(pair_in, tri_weight, me, group, samp_size, others):
    channels, height, keys = pair_in.shape
    share = channels // samp_size
    part = height // (group // share)
    rows = 16
    out = jax.ShapeDtypeStruct((group, part + height, keys), jnp.bfloat16)
    return pl.pallas_call(
        pair_project_kernel,
        grid=(height // rows,),
        out_shape=out,
        in_specs=[
            SCALAR,
            pl.BlockSpec((channels, rows, keys), lambda i: (0, i, 0)),
            whole(tri_weight.shape),
        ]
        + [UNREAD] * len(others),
        out_specs=whole(out.shape),
        scratch_shapes=[
            pltpu.VMEM((4 * share, channels), jnp.float32),
            pltpu.VMEM((channels * rows, keys), jnp.float32),
            pltpu.VMEM((share * height, keys), jnp.float32),
            pltpu.VMEM((share * height, keys), jnp.float32),
        ],
        compiler_params=pltpu.CompilerParams(vmem_limit_bytes=CLAIM * MIB),
        cost_estimate=expected(9.7),
        name="pair_project",
    )(me, pair_in, tri_weight, *others)


def pair_update_kernel(me_ref, came, own, gate_w, out_w, bias_w, *refs):
    back, message, rows_a, rows_b, rows_c = refs[-5:]
    channels, count, keys = came.shape
    over_rows = (((0,), (0,)), ((), ()))

    def by_channel(value, rows, first):
        height = value.shape[1]
        rows[...] = value.astype(jnp.float32).reshape(channels * height, keys)
        return jnp.concatenate(
            [rows[pl.ds(first + u, channels, stride=height), :] for u in range(count)], 1
        )

    def normed(value):
        return channel_norm(value, 0).astype(jnp.bfloat16)

    pair = by_channel(own[...], rows_a, lax.rem(me_ref[0], own.shape[1] // count) * count)
    sums = by_channel(came[...], rows_b, 0)
    gate = lax.dot_general(gate_w[0], normed(pair), over_rows, preferred_element_type=jnp.float32)
    update = lax.dot_general(out_w[...], normed(sums), over_rows, preferred_element_type=jnp.float32)
    new = (pair + jax.nn.sigmoid(gate) * update).astype(jnp.bfloat16).astype(jnp.float32)
    bias = jnp.dot(bias_w[...], normed(new), preferred_element_type=jnp.float32)
    for u in range(count):
        at = slice(u * keys, (u + 1) * keys)
        rows_b[pl.ds(u, channels, stride=count), :] = new[:, at]
        rows_c[pl.ds(u, bias.shape[0], stride=count), :] = bias[:, at]
    back[...] = rows_b[...].reshape(channels, count, keys).astype(jnp.bfloat16)
    _, cols, layers, heads = message.shape[:4]
    made = rows_c[...].reshape(layers, cols, heads, count, keys).astype(jnp.bfloat16)
    for k in range(message.shape[0]):
        for layer in range(layers):
            message[k, :, layer] = made[layer]


def pair_update(
    me, came, pair_in, tri_weight, out_weight, bias_w, layers, samp_size, col_size, others
):
    channels, count, keys = came.shape
    heads = bias_w.shape[0] // (layers * col_size)
    out_shape = (
        jax.ShapeDtypeStruct(came.shape, jnp.bfloat16),
        jax.ShapeDtypeStruct((samp_size, col_size, layers, heads, count, keys), jnp.bfloat16),
    )

    def fixed(shape, *at):
        return pl.BlockSpec(tuple(shape), lambda i, me: (at or (0,) * len(shape)))

    return pl.pallas_call(
        pair_update_kernel,
        grid_spec=pltpu.PrefetchScalarGridSpec(
            num_scalar_prefetch=1,
            grid=(1,),
            in_specs=[
                fixed(came.shape),
                pl.BlockSpec((channels, 2 * count, keys), lambda i, me: (0, me[0] // 2, 0)),
                fixed((1,) + tri_weight.shape[1:], 4, 0, 0),
                fixed(out_weight.shape),
                fixed(bias_w.shape),
            ]
            + [UNREAD] * len(others),
            out_specs=tuple(fixed(o.shape) for o in out_shape),
            scratch_shapes=[
                pltpu.VMEM((2 * channels * count, keys), jnp.float32),
                pltpu.VMEM((channels * count, keys), jnp.float32),
                pltpu.VMEM((bias_w.shape[0] * count, keys), jnp.float32),
            ],
        ),
        out_shape=out_shape,
        compiler_params=pltpu.CompilerParams(vmem_limit_bytes=CLAIM * MIB),
        cost_estimate=expected(2.8),
        name="pair_update",
    )(me, came, pair_in, tri_weight, out_weight, bias_w, *others)


def pair_rows_kernel(came, out):
    for c in range(came.shape[1]):
        rows = [came[k, c].astype(jnp.float32) for k in range(came.shape[0])]
        out[c] = jnp.concatenate(rows, 0).astype(jnp.bfloat16)


def pair_rows_joined(came):
    parts, share, count, keys = came.shape
    return local_call(
        pair_rows_kernel,
        jax.ShapeDtypeStruct((share, parts * count, keys), jnp.bfloat16),
        [whole(came.shape)],
        [came],
        [],
        1.7,
        "pair_rows",
    )


def body(
    pair_in,
    token_act,
    single,
    noise_sigma,
    token_mask,
    tri_weight,
    out_weight,
    bias_weight,
    time_weight,
    mod_weight,
    query_weight,
    key_weight,
    value_gate_weight,
    attn_out_weight,
    up_weight,
    down_weight,
):
    channels, pair_rows, pair_cols = pair_in.shape
    samp_size, row_size, col_size = (lax.axis_size(name) for name in ("samp", "row", "col"))
    group = row_size * col_size
    share = channels // samp_size
    halves = group // share
    half_rows = pair_rows // halves
    cell_rows = half_rows // samp_size
    own_rows = halves * cell_rows
    samp_at = jnp.reshape(lax.axis_index("samp"), (1,))
    row_at = jnp.reshape(lax.axis_index("row"), (1,))
    col_at = jnp.reshape(lax.axis_index("col"), (1,))
    blocks, _, head_count = bias_weight.shape

    state = jnp.swapaxes(token_act, 1, 2)
    samples, width, row_count = state.shape
    wide = state.astype(jnp.float32)
    sums = jnp.stack([jnp.sum(wide, 1), jnp.sum(wide * wide, 1)])
    sums = sum(swap_all(sums, "col"))
    query_w = jnp.swapaxes(query_weight, 1, 2)
    key_w = jnp.swapaxes(key_weight, 1, 2)
    value_gate_w = jnp.swapaxes(value_gate_weight, 2, 3)
    mod_w = jnp.swapaxes(mod_weight, 2, 3)
    half_count = TEMB // 2
    frequency = jnp.exp(jnp.arange(half_count, dtype=jnp.float32) * (math.log(100.0) / half_count))
    angles = (jnp.log(noise_sigma) * 0.25)[:, None] * frequency[None, :]
    time_embed = jnp.concatenate([jnp.cos(angles), jnp.sin(angles)], 1).astype(jnp.bfloat16)

    to_send = pair_project(pair_in, tri_weight, samp_at, group, samp_size, [sums, time_embed])
    came = lax.all_to_all(to_send, ("row", "col"), 0, 0, tiled=True)
    came = came.reshape(row_size, col_size, half_rows + pair_rows, pair_cols)

    attn_local, trans_local, mods, later, shared = modulate(
        single, time_embed, time_weight, mod_w, state, sums, [to_send]
    )

    attn_full = swap_all(attn_local, "col")
    triangle = triangle_sums(came, attn_full[1:])
    shared = swap_all(shared, "col")
    triangle = triangle.reshape(samp_size * group, cell_rows, pair_cols)
    triangle = lax.all_to_all(triangle, ("samp", "row", "col"), 0, 0, tiled=True)
    triangle = triangle.reshape(channels, own_rows, pair_cols)
    mask_row = token_mask[None]
    queries, gates, both = project(
        attn_full, col_at, query_w, key_w, value_gate_w, mask_row, 0
    )
    pieces = swap_all(both, "row")

    trans_full = swap_all(trans_local, "col")

    bias_w = jnp.swapaxes(bias_weight, 1, 2).reshape(blocks * head_count, channels)
    pair_out, bias = pair_update(
        samp_at,
        triangle,
        pair_in,
        tri_weight,
        out_weight,
        bias_w,
        blocks,
        samp_size // NEAR,
        col_size,
        [both, *trans_full[1:]],
    )
    far = samp_size // NEAR
    message = bias.shape
    bias = lax.all_to_all(
        bias.reshape((far * col_size,) + message[2:]),
        ("samp", "col"),
        0,
        0,
        axis_index_groups=[
            [(z * NEAR + x) * col_size + c for z in range(far) for c in range(col_size)]
            for x in range(NEAR)
        ],
        tiled=True,
    ).reshape(message)
    biases = [bias] + [
        lax.ppermute(bias, "samp", [(k, k ^ flip) for k in range(samp_size)])
        for flip in range(1, NEAR)
    ]
    pair_back = after(pair_out, [biases[1]]).reshape(samp_size, share, own_rows, pair_cols)
    pair_back = lax.all_to_all(pair_back, "samp", 0, 0, tiled=True)
    trans = transition(trans_full, col_at, up_weight, down_weight, 0, col_size)
    trans_sum, sent = sum_parts(*trans)
    seat = jnp.concatenate([row_at, samp_at % NEAR, col_at])

    for layer in range(blocks):
        if layer > 0:
            queries, gates, both, trans_local = project(
                [state], col_at, query_w, key_w, value_gate_w, mask_row, layer, shared, later
            )
            pieces = swap_all(both, "row")
            trans_full = swap_all(trans_local, "col")
            trans = transition(trans_full, col_at, up_weight, down_weight, layer, col_size)
            trans_sum, sent = sum_parts(*trans)
        others = [sent] if layer else [trans_sum[2], *shared[1:]]
        attended = attention(
            seat, queries, gates, pieces, biases, attn_out_weight, layer, others
        )
        state = finish(
            sum_parts(*attended)[0], trans_sum, mods, 2 * layer, [] if layer else [pair_back]
        )
        if layer == 0:
            state = lax.all_gather(state, "col", axis=0)
    pair_back = pair_rows_joined(pair_back)
    return (pair_back, jnp.swapaxes(state, 1, 2))


def solution(mesh):
    placed = (
        P(None, "row", "col"),
        P("samp", "row", "col"),
        P("row", None),
        P("samp"),
        P("row"),
        P(),
        P(),
        P(),
        P(),
        P(None, None, None, "col"),
        P(None, None, "col"),
        P(None, None, "col"),
        P(None, None, None, "col"),
        P(None, "col", None),
        P(None, None, None, "col"),
        P(None, "col", None),
    )
    return jax.shard_map(
        body,
        mesh=mesh,
        in_specs=placed,
        out_specs=(P("samp", "row", "col"), P("samp", "row", "col")),
        check_vma=False,
    )
```

```python
import math

import jax
import jax.numpy as jnp
from jax import lax
from jax.experimental import pallas as pl
from jax.experimental.pallas import tpu as pltpu
from jax.sharding import PartitionSpec as P

DA = 768
HEAD_DIM = 48
TEMB = 256


EPS = 1e-05
MASK_FILL = 1000000000.0
MIB = 1024 * 1024
CLAIM = 64 * MIB - 64 * 1024
MASK_ROWS = 16
NEAR = 4


def channel_norm(values, axis):
    mean_value = jnp.mean(values, axis=axis, keepdims=True)
    centred = values - mean_value
    spread = jnp.mean(centred * centred, axis=axis, keepdims=True)
    return centred * lax.rsqrt(spread + EPS)


def swap(value, axis, flip):
    size = lax.axis_size(axis)
    return lax.ppermute(value, axis, [(k, k ^ flip) for k in range(size)])


def swap_all(value, axis):
    return [value] + [swap(value, axis, flip) for flip in range(1, lax.axis_size(axis))]


def expected(micros):
    return pl.CostEstimate(flops=0, bytes_accessed=int(micros * 3.69e6), transcendentals=0)


def local_call(kernel, out_shape, in_specs, args, scratch, micros, name):
    return pl.pallas_call(
        kernel,
        grid=(1,),
        out_shape=out_shape,
        in_specs=in_specs,
        out_specs=jax.tree.map(lambda o: whole(o.shape), out_shape),
        scratch_shapes=scratch,
        compiler_params=pltpu.CompilerParams(vmem_limit_bytes=CLAIM),
        cost_estimate=expected(micros),
        name=name,
    )(*args)


def whole(shape):
    return pl.BlockSpec(tuple(shape), lambda i: (0,) * len(shape))


def layer_block(shape, at, layer):
    block = tuple(1 if d == at else n for d, n in enumerate(shape))
    return pl.BlockSpec(block, lambda i: tuple(layer if d == at else 0 for d in range(len(shape))))


SCALAR = pl.BlockSpec(memory_space=pltpu.SMEM)
UNREAD = pl.BlockSpec(memory_space=pl.ANY)


def after(value, others):
    return pl.pallas_call(
        lambda *refs: None,
        out_shape=jax.ShapeDtypeStruct(value.shape, value.dtype),
        in_specs=[UNREAD] * (1 + len(others)),
        out_specs=UNREAD,
        input_output_aliases={0: 0},
        name="after",
    )(value, *others)


def stack_gathered(gathered, full):
    parts, samples, width, tokens = gathered.shape
    for k in range(parts):
        for s in range(samples):
            full[k * width : (k + 1) * width, s * tokens : (s + 1) * tokens] = gathered[k, s]


def stack_normed(me, gathered, shared, own, full, normed, trans):
    parts, samples, width, tokens = gathered.shape
    for s in range(samples):
        at = slice(s * tokens, (s + 1) * tokens)
        value = jnp.concatenate([gathered[k, s] for k in range(parts)], 0).astype(jnp.float32)
        normed[...] = channel_norm(value, 0)
        for k, pair in enumerate(shared):
            rows = pl.ds(pl.multiple_of((me ^ k) * width, width), width)
            value = normed[rows, :]
            gain, shift = pair[0, s].astype(jnp.float32), pair[1, s].astype(jnp.float32)
            full[rows, at] = (gain * value + shift).astype(jnp.bfloat16)
            if k == 0:
                gain, shift = own[0, s].astype(jnp.float32), own[1, s].astype(jnp.float32)
                trans[s] = (gain * value + shift).astype(jnp.bfloat16)


def first_project_kernel(gathered, *refs):
    stack_gathered(gathered, refs[-1])
    project_full(*refs)


def later_project_kernel(me_ref, gathered, pair0, pair1, pair2, pair3, own, *refs):
    *rest, trans, full, normed = refs
    shared = (pair0, pair1, pair2, pair3)
    stack_normed(me_ref[0], gathered, shared, own, full, normed, trans)
    project_full(*rest, full)


def project_full(query_w, key_w, value_gate_w, mask, queries, gates, both, full):
    samples, width, tokens = queries.shape

    def times(weight):
        return jnp.dot(weight, full[...], preferred_element_type=jnp.float32).astype(jnp.bfloat16)

    key, value = times(key_w[0]), times(value_gate_w[0, 0])
    query, gate = times(query_w[0]), times(value_gate_w[0, 1])
    for s in range(samples):
        at = slice(s * tokens, (s + 1) * tokens)
        queries[s] = query[:, at]
        gates[s] = gate[:, at]
        both[2 * s * width : (2 * s + 1) * width] = key[:, at]
        both[(2 * s + 1) * width : (2 * s + 2) * width] = value[:, at]
    both[2 * samples * width :] = jnp.broadcast_to(
        mask[...].astype(jnp.float32), (MASK_ROWS, tokens)
    ).astype(jnp.bfloat16)


def project(blocks, me, query_w, key_w, value_gate_w, mask, layer, shared=None, own=None):
    samples, width, tokens = blocks[0].shape[-3:]
    small = jax.ShapeDtypeStruct((samples, width, tokens), jnp.bfloat16)
    joint = jax.ShapeDtypeStruct((2 * samples * width + MASK_ROWS, tokens), jnp.bfloat16)
    specs = [
        layer_block(query_w.shape, 0, layer),
        layer_block(key_w.shape, 0, layer),
        layer_block(value_gate_w.shape, 0, layer),
        whole(mask.shape),
    ]
    args = [query_w, key_w, value_gate_w, mask]
    depth = query_w.shape[2]
    full = pltpu.VMEM((depth, samples * tokens), jnp.bfloat16)
    if shared is None:
        return local_call(
            first_project_kernel,
            (small, small, joint),
            [whole(blocks[0].shape)] + specs,
            [*blocks, *args],
            [full],
            3.0,
            "first_project",
        )
    return local_call(
        later_project_kernel,
        (small, small, joint, small),
        [SCALAR] + [whole(a.shape) for a in (*blocks, *shared, own)] + specs,
        [me, *blocks, *shared, own, *args],
        [full, pltpu.VMEM((depth, tokens), jnp.float32)],
        4.0,
        "later_project",
    )


def mod_block(mods, m):
    return pl.BlockSpec((1,) + mods.shape[1:], lambda i: (m, 0, 0, 0))


def hand_out(total, me, keep, give):
    samples, width, tokens = keep.shape[1:]
    for e in range(keep.shape[0]):
        for target, flip in ((keep, 2 * e), (give, 2 * e + 1)):
            start = pl.multiple_of((me ^ flip) * width, width)
            for s in range(samples):
                piece = total[pl.ds(start, width), s * tokens : (s + 1) * tokens]
                target[e, s] = piece.astype(target.dtype)


def join_kernel(keep, came, out):
    out[...] = (keep[0] + came[0].astype(jnp.float32)).astype(out.dtype)


def sum_parts(keep, give):
    came = swap(give, "col", 1)
    far = local_call(
        join_kernel,
        jax.ShapeDtypeStruct(keep.shape[1:], jnp.bfloat16),
        [pl.BlockSpec((1,) + keep.shape[1:], lambda i: (1, 0, 0, 0))] * 2,
        [keep, came],
        [],
        1.0,
        "join",
    )
    return [keep, came, swap(far, "col", 2)], far


def stack_features(blocks, full, me):
    for k, block in enumerate(blocks):
        samples, width, tokens = block.shape
        start = pl.multiple_of((me ^ k) * width, width)
        for s in range(samples):
            full[pl.ds(start, width), s * tokens : (s + 1) * tokens] = block[s]


def transition_kernel(count, me_ref, *refs):
    up, down = refs[count : count + 2]
    keep, give, full, total = refs[-4:]
    if count > 1:
        stack_features(refs[:count], full, me_ref[0])
    else:
        stack_gathered(refs[0], full)
    over_rows = (((0,), (0,)), ((), ()))
    swish = lax.dot_general(up[0, 0], full[...], over_rows, preferred_element_type=jnp.float32)
    linear = lax.dot_general(up[0, 1], full[...], over_rows, preferred_element_type=jnp.float32)
    hidden = (swish / (1.0 + jnp.exp(-swish)) * linear).astype(jnp.bfloat16)
    total[...] = lax.dot_general(down[0], hidden, over_rows, preferred_element_type=jnp.float32)
    hand_out(total, me_ref[0], keep, give)


def transition(blocks, me, up, down, layer, col_size, others):
    samples, width, tokens = blocks[0].shape[-3:]
    depth, hidden = up.shape[2:]
    return local_call(
        lambda *refs: transition_kernel(len(blocks), *refs),
        tuple(
            jax.ShapeDtypeStruct((col_size // 2, samples, width, tokens), dtype)
            for dtype in (jnp.float32, jnp.bfloat16)
        ),
        [SCALAR]
        + [whole(b.shape) for b in blocks]
        + [layer_block(up.shape, 0, layer), layer_block(down.shape, 0, layer)]
        + [UNREAD] * len(others),
        [me, *blocks, up, down, *others],
        [
            pltpu.VMEM((depth, samples * tokens), jnp.bfloat16),
            pltpu.VMEM((depth, samples * tokens), jnp.float32),
        ],
        3.8,
        "transition",
    )


def attention_kernel(row_ref, samp_ref, col_ref, queries, gates, kv0, kv1, kv2, kv3, bias0, bias1, bias2, bias3, *refs):
    out_w, keep, give, full, total, added = refs[0], *refs[-5:]
    pieces, biases = (kv0, kv1, kv2, kv3), (bias0, bias1, bias2, bias3)
    row_at, near_at, col_at = row_ref[0], lax.rem(samp_ref[0], NEAR), col_ref[0]
    samples, width, tokens = queries.shape
    far, cols, _, heads, count, keys = bias0.shape
    for k, bias in enumerate(biases):
        for z in range(far):
            start = pl.multiple_of((z * len(biases) + (near_at ^ k)) * count, count)
            for j in range(cols):
                added[:, pl.ds(start, count), j * keys : (j + 1) * keys] = bias[
                    z, row_at ^ j, 0
                ].astype(jnp.float32)
    scale = 1.0 / math.sqrt(HEAD_DIM)
    lane = lax.broadcasted_iota(jnp.int32, (tokens, width), 1) // HEAD_DIM
    masks = jnp.concatenate(
        [kv[2 * samples * width : 2 * samples * width + 1].astype(jnp.float32) for kv in pieces], 1
    )
    mask_add = (masks - 1.0) * MASK_FILL
    for s in range(samples):
        query = jnp.transpose(queries[s].astype(jnp.float32))
        key = jnp.concatenate([kv[2 * s * width : (2 * s + 1) * width] for kv in pieces], 1)
        value = jnp.concatenate([kv[(2 * s + 1) * width : (2 * s + 2) * width] for kv in pieces], 1)
        stacked = jnp.concatenate([jnp.where(lane == h, query, 0.0) for h in range(heads)], 0)
        scores = jnp.dot(stacked.astype(jnp.bfloat16), key, preferred_element_type=jnp.float32)
        scores = scores * scale + added[...].reshape(scores.shape) + mask_add
        exps = jnp.exp(scores - jnp.max(scores, axis=1, keepdims=True))
        norm = jnp.sum(exps, axis=1, keepdims=True)
        product = lax.dot_general(
            exps.astype(jnp.bfloat16),
            value,
            (((1,), (1,)), ((), ())),
            preferred_element_type=jnp.float32,
        )
        product = product / norm
        kept = product[:tokens]
        for h in range(1, heads):
            kept = jnp.where(lane == h, product[h * tokens : (h + 1) * tokens], kept)
        gate = jax.nn.sigmoid(gates[s].astype(jnp.float32))
        full[:, s * tokens : (s + 1) * tokens] = (gate * jnp.transpose(kept)).astype(jnp.bfloat16)
    total[...] = lax.dot_general(
        out_w[0], full[...], (((0,), (0,)), ((), ())), preferred_element_type=jnp.float32
    )
    hand_out(total, col_at, keep, give)


def attention(me, queries, gates, pieces, biases, out_w, layer, others):
    samples, width, tokens = queries.shape
    heads = biases[0].shape[3]
    parts = out_w.shape[2] // width
    args = [queries, gates, *pieces]
    return local_call(
        attention_kernel,
        tuple(
            jax.ShapeDtypeStruct((parts // 2,) + queries.shape, dtype)
            for dtype in (jnp.float32, jnp.bfloat16)
        ),
        [SCALAR] * len(me)
        + [whole(a.shape) for a in args]
        + [layer_block(b.shape, 2, layer) for b in biases]
        + [layer_block(out_w.shape, 0, layer)]
        + [UNREAD] * len(others),
        [*me, *args, *biases, out_w, *others],
        [
            pltpu.VMEM((width, samples * tokens), jnp.bfloat16),
            pltpu.VMEM((parts * width, samples * tokens), jnp.float32),
            pltpu.VMEM((heads, tokens, len(pieces) * tokens), jnp.float32),
        ],
        5.4,
        "attention",
    )


def finish_kernel(keep_a, came_a, far_a, keep_t, came_t, far_t, gate_a, gate_t, *refs):
    state = refs[-1]
    for s in range(state.shape[0]):
        branch, trans = (
            keep[0, s] + came[0, s].astype(jnp.float32) + far[s].astype(jnp.float32)
            for keep, came, far in ((keep_a, came_a, far_a), (keep_t, came_t, far_t))
        )
        value = gate_a[0, s].astype(jnp.float32) * branch + gate_t[0, s].astype(jnp.float32) * trans
        state[s] = value.astype(state.dtype)


def finish(attended, trans, mods, gate_at, others):
    block = mods.shape[1:]
    first = pl.BlockSpec((1,) + block, lambda i: (0, 0, 0, 0))
    return local_call(
        finish_kernel,
        jax.ShapeDtypeStruct(block, jnp.bfloat16),
        [first, first, whole(block)] * 2
        + [mod_block(mods, gate_at), mod_block(mods, gate_at + 1)]
        + [UNREAD] * len(others),
        [*attended, *trans, mods, mods, *others],
        [],
        2.0,
        "finish",
    )


def modulate_kernel(single, time_embed, time_w, mod_w, state, sums, *refs):
    attn, trans, gates, later, shared, normed = refs[-6:]
    samples, width, tokens = state.shape
    layers, count = mod_w.shape[:2]
    shift = jnp.dot(time_embed[...], time_w[...], preferred_element_type=jnp.float32)
    for s in range(samples):
        condition = single[...].astype(jnp.float32) + shift[s : s + 1, :]
        normed[s * tokens : (s + 1) * tokens] = channel_norm(condition, 1).astype(jnp.bfloat16)

    def made(layer, m):
        value = lax.dot_general(
            mod_w[layer, m],
            normed[...],
            (((1,), (1,)), ((), ())),
            preferred_element_type=jnp.float32,
        )
        value = value if m in (1, 3) else jax.nn.sigmoid(value)
        return [value[:, s * tokens : (s + 1) * tokens] for s in range(samples)]

    mean_value = sums[0] / DA
    scale = lax.rsqrt(sums[1] / DA - mean_value * mean_value + EPS)
    for target, m in ((attn, 0), (trans, 2)):
        gain, shift = made(0, m), made(0, m + 1)
        for s in range(samples):
            value = (state[s].astype(jnp.float32) - mean_value[s : s + 1]) * scale[s : s + 1]
            target[s] = (gain[s] * value + shift[s]).astype(jnp.bfloat16)
    for layer in range(layers):
        for m in range(4, count):
            for s, value in enumerate(made(layer, m)):
                gates[layer * (count - 4) + m - 4, s] = value.astype(jnp.bfloat16)
    for m in range(4):
        for s, value in enumerate(made(layers - 1, m)):
            target = shared if m < 2 else later
            target[m % 2, s] = value.astype(jnp.bfloat16)


def modulate(single, time_embed, time_w, mod_w, state, sums, others):
    layers, count, _, depth = mod_w.shape
    samples, _, tokens = state.shape
    args = [single, time_embed, time_w, mod_w, state, sums]
    return local_call(
        modulate_kernel,
        tuple(
            jax.ShapeDtypeStruct(lead + state.shape, jnp.bfloat16)
            for lead in ((), (), (2 * layers,), (2,), (2,))
        ),
        [whole(a.shape) for a in args] + [UNREAD] * len(others),
        args + others,
        [pltpu.VMEM((samples * tokens, depth), jnp.bfloat16)],
        4.5,
        "modulate",
    )


def triangle_kernel(came, *refs):
    out = refs[-1]
    rows, cols, _, keys = came.shape
    half = 8 * out.shape[0]

    def joined(at):
        return jnp.concatenate(
            [jnp.concatenate([came[r, c, at] for c in range(cols)], 1) for r in range(rows)], 0
        )

    sums = lax.dot_general(
        joined(slice(0, half)),
        joined(slice(half, half + keys)),
        (((1,), (1,)), ((), ())),
        preferred_element_type=jnp.float32,
    )
    groups = half // 8
    upper = lax.broadcasted_iota(jnp.int32, (groups, 8, keys), 1) < 4
    for r in range(rows):
        for c in range(0, cols, 2):
            one, two = (
                sums[r * half : (r + 1) * half, k * keys : (k + 1) * keys].reshape(groups, 8, keys)
                for k in (c, c + 1)
            )
            even = jnp.where(upper, one, pltpu.roll(two, 4, 1))
            odd = jnp.where(upper, pltpu.roll(one, 4, 1), two)
            out[:, 0, r, c // 2] = even.astype(jnp.bfloat16)
            out[:, 1, r, c // 2] = odd.astype(jnp.bfloat16)


def triangle_sums(came, others):
    rows, cols, height, keys = came.shape
    half = height - keys
    left = rows * half
    return local_call(
        triangle_kernel,
        jax.ShapeDtypeStruct((half // 8, 2, rows, cols // 2, 8, keys), jnp.bfloat16),
        [whole(came.shape)] + [UNREAD] * len(others),
        [came, *others],
        [],
        2.2,
        "triangle_sums",
    )


def pair_project_kernel(me_ref, pair, tri, *refs):
    out, weight, normed, left, right = refs[-5:]
    step = pl.program_id(0)
    channels, rows, keys = pair.shape
    height = rows * pl.num_programs(0)
    share = weight.shape[0] // 4
    halves = out.shape[0] // share
    part = out.shape[1] - keys
    group = 8 // halves

    @pl.when(step == 0)
    def _():
        mine = lax.broadcasted_iota(jnp.int32, (share, channels), 0) + me_ref[0] * share
        pick = mine == lax.broadcasted_iota(jnp.int32, (share, channels), 1)
        for p in range(4):
            weight[p * share : (p + 1) * share] = lax.dot_general(
                pick.astype(jnp.bfloat16),
                tri[p],
                (((1,), (1,)), ((), ())),
                preferred_element_type=jnp.float32,
            )

    def over_channels(term):
        lanes = [term(c) for c in range(4)]
        for c in range(4, channels):
            lanes[c % 4] = lanes[c % 4] + term(c)
        return (lanes[0] + lanes[1] + (lanes[2] + lanes[3])) / channels

    mean_value = over_channels(lambda c: pair[c].astype(jnp.float32))
    spread = over_channels(lambda c: jnp.square(pair[c].astype(jnp.float32) - mean_value))
    scale = lax.rsqrt(spread + EPS)
    for c in range(channels):
        normed[c * rows : (c + 1) * rows] = (pair[c].astype(jnp.float32) - mean_value) * scale
    weights = weight[...].astype(jnp.bfloat16)
    for i in range(0, rows, 2):
        two = [normed[pl.ds(i + e, channels, stride=rows), :] for e in (0, 1)]
        made = jnp.dot(
            weights, jnp.concatenate(two, 1).astype(jnp.bfloat16), preferred_element_type=jnp.float32
        )
        made_left = jax.nn.sigmoid(made[:share]) * made[share : 2 * share]
        made_right = jax.nn.sigmoid(made[2 * share : 3 * share]) * made[3 * share :]
        for e in (0, 1):
            row, at = i + e, slice(e * keys, (e + 1) * keys)
            right[pl.ds(step * rows + row, share, stride=keys), :] = made_right[:, at]
            place = (row % 8) // group * part + row // 8 * group + row % group
            place = step * (rows // 8 * group) + place
            left[pl.ds(place, share, stride=keys), :] = made_left[:, at]

    @pl.when(step == pl.num_programs(0) - 1)
    def _():
        for c in range(share):
            whole_right = right[c * keys : (c + 1) * keys].astype(jnp.bfloat16)
            for h in range(halves):
                start = c * keys + h * part
                out[c * halves + h, :part] = left[start : start + part].astype(jnp.bfloat16)
                out[c * halves + h, part:] = whole_right


def pair_project(pair_in, tri_weight, me, group, samp_size, others):
    channels, height, keys = pair_in.shape
    share = channels // samp_size
    part = height // (group // share)
    rows = 16
    out = jax.ShapeDtypeStruct((group, part + height, keys), jnp.bfloat16)
    return pl.pallas_call(
        pair_project_kernel,
        grid=(height // rows,),
        out_shape=out,
        in_specs=[
            SCALAR,
            pl.BlockSpec((channels, rows, keys), lambda i: (0, i, 0)),
            whole(tri_weight.shape),
        ]
        + [UNREAD] * len(others),
        out_specs=whole(out.shape),
        scratch_shapes=[
            pltpu.VMEM((4 * share, channels), jnp.float32),
            pltpu.VMEM((channels * rows, keys), jnp.float32),
            pltpu.VMEM((share * height, keys), jnp.float32),
            pltpu.VMEM((share * height, keys), jnp.float32),
        ],
        compiler_params=pltpu.CompilerParams(vmem_limit_bytes=CLAIM),
        cost_estimate=expected(9.7),
        name="pair_project",
    )(me, pair_in, tri_weight, *others)


def pair_update_kernel(me_ref, came, own, gate_w, out_w, bias_w, *refs):
    back, message, rows_a, rows_b, rows_c = refs[-5:]
    channels, count, keys = came.shape
    over_rows = (((0,), (0,)), ((), ()))

    def by_channel(value, rows, first):
        height = value.shape[1]
        rows[...] = value.astype(jnp.float32).reshape(channels * height, keys)
        return jnp.concatenate(
            [rows[pl.ds(first + u, channels, stride=height), :] for u in range(count)], 1
        )

    def normed(value):
        return channel_norm(value, 0).astype(jnp.bfloat16)

    pair = by_channel(own[...], rows_a, lax.rem(me_ref[0], own.shape[1] // count) * count)
    sums = by_channel(came[...], rows_b, 0)
    gate = lax.dot_general(gate_w[0], normed(pair), over_rows, preferred_element_type=jnp.float32)
    update = lax.dot_general(out_w[...], normed(sums), over_rows, preferred_element_type=jnp.float32)
    new = (pair + jax.nn.sigmoid(gate) * update).astype(jnp.bfloat16).astype(jnp.float32)
    bias = jnp.dot(bias_w[...], normed(new), preferred_element_type=jnp.float32)
    for u in range(count):
        at = slice(u * keys, (u + 1) * keys)
        rows_b[pl.ds(u, channels, stride=count), :] = new[:, at]
        rows_c[pl.ds(u, bias.shape[0], stride=count), :] = bias[:, at]
    back[...] = rows_b[...].reshape(channels, count, keys).astype(jnp.bfloat16)
    _, cols, layers, heads = message.shape[:4]
    made = rows_c[...].reshape(layers, cols, heads, count, keys).astype(jnp.bfloat16)
    for k in range(message.shape[0]):
        for layer in range(layers):
            message[k, :, layer] = made[layer]


def pair_update(
    me, came, pair_in, tri_weight, out_weight, bias_w, layers, samp_size, col_size, others
):
    channels, count, keys = came.shape
    heads = bias_w.shape[0] // (layers * col_size)
    out_shape = (
        jax.ShapeDtypeStruct(came.shape, jnp.bfloat16),
        jax.ShapeDtypeStruct((samp_size, col_size, layers, heads, count, keys), jnp.bfloat16),
    )

    def fixed(shape, *at):
        return pl.BlockSpec(tuple(shape), lambda i, me: (at or (0,) * len(shape)))

    return pl.pallas_call(
        pair_update_kernel,
        grid_spec=pltpu.PrefetchScalarGridSpec(
            num_scalar_prefetch=1,
            grid=(1,),
            in_specs=[
                fixed(came.shape),
                pl.BlockSpec((channels, 2 * count, keys), lambda i, me: (0, me[0] // 2, 0)),
                fixed((1,) + tri_weight.shape[1:], 4, 0, 0),
                fixed(out_weight.shape),
                fixed(bias_w.shape),
            ]
            + [UNREAD] * len(others),
            out_specs=tuple(fixed(o.shape) for o in out_shape),
            scratch_shapes=[
                pltpu.VMEM((2 * channels * count, keys), jnp.float32),
                pltpu.VMEM((channels * count, keys), jnp.float32),
                pltpu.VMEM((bias_w.shape[0] * count, keys), jnp.float32),
            ],
        ),
        out_shape=out_shape,
        compiler_params=pltpu.CompilerParams(vmem_limit_bytes=CLAIM),
        cost_estimate=expected(2.8),
        name="pair_update",
    )(me, came, pair_in, tri_weight, out_weight, bias_w, *others)


def pair_rows_kernel(came, out):
    for c in range(came.shape[1]):
        rows = [came[k, c].astype(jnp.float32) for k in range(came.shape[0])]
        out[c] = jnp.concatenate(rows, 0).astype(jnp.bfloat16)


def pair_rows_joined(came):
    parts, share, count, keys = came.shape
    return local_call(
        pair_rows_kernel,
        jax.ShapeDtypeStruct((share, parts * count, keys), jnp.bfloat16),
        [whole(came.shape)],
        [came],
        [],
        1.7,
        "pair_rows",
    )


def body(
    pair_in,
    token_act,
    single,
    noise_sigma,
    token_mask,
    tri_weight,
    out_weight,
    bias_weight,
    time_weight,
    mod_weight,
    query_weight,
    key_weight,
    value_gate_weight,
    attn_out_weight,
    up_weight,
    down_weight,
):
    channels, pair_rows, pair_cols = pair_in.shape
    samp_size, row_size, col_size = (lax.axis_size(name) for name in ("samp", "row", "col"))
    group = row_size * col_size
    share = channels // samp_size
    halves = group // share
    half_rows = pair_rows // halves
    cell_rows = half_rows // samp_size
    own_rows = halves * cell_rows
    samp_at = jnp.reshape(lax.axis_index("samp"), (1,))
    row_at = jnp.reshape(lax.axis_index("row"), (1,))
    col_at = jnp.reshape(lax.axis_index("col"), (1,))
    blocks, _, head_count = bias_weight.shape

    state = jnp.swapaxes(token_act, 1, 2)
    samples, width, row_count = state.shape
    wide = state.astype(jnp.float32)
    sums = jnp.stack([jnp.sum(wide, 1), jnp.sum(wide * wide, 1)])
    sums = sum(swap_all(sums, "col"))
    query_w = jnp.swapaxes(query_weight, 1, 2)
    key_w = jnp.swapaxes(key_weight, 1, 2)
    value_gate_w = jnp.swapaxes(value_gate_weight, 2, 3)
    mod_w = jnp.swapaxes(mod_weight, 2, 3)
    half_count = TEMB // 2
    frequency = jnp.exp(jnp.arange(half_count, dtype=jnp.float32) * (math.log(100.0) / half_count))
    angles = (jnp.log(noise_sigma) * 0.25)[:, None] * frequency[None, :]
    time_embed = jnp.concatenate([jnp.cos(angles), jnp.sin(angles)], 1).astype(jnp.bfloat16)

    to_send = pair_project(pair_in, tri_weight, samp_at, group, samp_size, [sums, time_embed])
    came = lax.all_to_all(to_send, ("row", "col"), 0, 0, tiled=True)
    came = came.reshape(row_size, col_size, half_rows + pair_rows, pair_cols)

    attn_local, trans_local, mods, later, shared = modulate(
        single, time_embed, time_weight, mod_w, state, sums, [to_send]
    )

    attn_full = lax.all_gather(attn_local, "col", axis=0)
    triangle = triangle_sums(came, [attn_full])
    shared = swap_all(shared, "col")
    triangle = triangle.reshape(samp_size * group, cell_rows, pair_cols)
    triangle = lax.all_to_all(triangle, ("samp", "row", "col"), 0, 0, tiled=True)
    triangle = triangle.reshape(channels, own_rows, pair_cols)
    mask_row = token_mask[None]
    queries, gates, both = project(
        [attn_full], col_at, query_w, key_w, value_gate_w, mask_row, 0
    )
    pieces = swap_all(both, "row")

    trans_full = swap_all(trans_local, "col")

    bias_w = jnp.swapaxes(bias_weight, 1, 2).reshape(blocks * head_count, channels)
    pair_out, bias = pair_update(
        samp_at,
        triangle,
        pair_in,
        tri_weight,
        out_weight,
        bias_w,
        blocks,
        samp_size // NEAR,
        col_size,
        [both, *trans_full[1:]],
    )
    far = samp_size // NEAR
    message = bias.shape
    bias = lax.all_to_all(
        bias.reshape((far * col_size,) + message[2:]),
        ("samp", "col"),
        0,
        0,
        axis_index_groups=[
            [(z * NEAR + x) * col_size + c for z in range(far) for c in range(col_size)]
            for x in range(NEAR)
        ],
        tiled=True,
    ).reshape(message)
    biases = [bias] + [
        lax.ppermute(bias, "samp", [(k, k ^ flip) for k in range(samp_size)])
        for flip in range(1, NEAR)
    ]
    pair_back = after(pair_out, [biases[1]]).reshape(samp_size, share, own_rows, pair_cols)
    pair_back = lax.all_to_all(pair_back, "samp", 0, 0, tiled=True)
    trans = transition(trans_full, col_at, up_weight, down_weight, 0, col_size, [])
    trans_sum, sent = sum_parts(*trans)
    seat = [row_at, samp_at, col_at]

    for layer in range(blocks):
        if layer > 0:
            queries, gates, both, trans_local = project(
                [state], col_at, query_w, key_w, value_gate_w, mask_row, layer, shared, later
            )
            pieces = swap_all(both, "row")
            trans_full = swap_all(trans_local, "col")
            trans = transition(
                trans_full, col_at, up_weight, down_weight, layer, col_size, pieces[1:2]
            )
            trans_sum, sent = sum_parts(*trans)
        others = [sent] if layer else [trans_sum[2], *shared[1:]]
        attended = attention(
            seat, queries, gates, pieces, biases, attn_out_weight, layer, others
        )
        state = finish(
            sum_parts(*attended)[0], trans_sum, mods, 2 * layer, [] if layer else [pair_back]
        )
        if layer == 0:
            state = lax.all_gather(state, "col", axis=0)
    pair_back = pair_rows_joined(pair_back)
    return (pair_back, jnp.swapaxes(state, 1, 2))


def solution(mesh):
    placed = (
        P(None, "row", "col"),
        P("samp", "row", "col"),
        P("row", None),
        P("samp"),
        P("row"),
        P(),
        P(),
        P(),
        P(),
        P(None, None, None, "col"),
        P(None, None, "col"),
        P(None, None, "col"),
        P(None, None, None, "col"),
        P(None, "col", None),
        P(None, None, None, "col"),
        P(None, "col", None),
    )
    return jax.shard_map(
        body,
        mesh=mesh,
        in_specs=placed,
        out_specs=(P("samp", "row", "col"), P("samp", "row", "col")),
        check_vma=False,
    )
```
